32 devices in a mesh: row: 4 (over y, x), col: 8 (over z, core).
Axes of the slice: x: 2, y: 2, z: 4, core: 2. Of those that a mesh axis runs over, the one named last changes fastest.
Arguments:
- scen_inverse: bfloat16 [64, 512, 512], P(('row', 'col')), may hold values from -32 to 32, as said below
- coupling: bfloat16 [64, 512, 3072], P(('row', 'col')), may hold values from -0.0625 to 0.0625
- scen_cot: bfloat16 [64, 512, 256], P(('row', 'col')), may hold values from -6 to 6
- first_cot: float32 [3072, 256], P('row'), may hold values from -6 to 6
- schur_inverse: float32 [3072, 3072], P('row', 'col'), may hold values from -32 to 32, as said below
- scen_primal: bfloat16 [64, 512, 256], P(('row', 'col')), may hold values from -0.375 to 0.375
- first_primal: bfloat16 [3072, 256], replicated, may hold values from -0.375 to 0.375
Outputs:
- scen_adjoint: float32 [64, 512, 256], P(('row', 'col'))
- first_adjoint: float32 [3072, 256], P('col')
- coupling_grad: float32 [64, 512, 3072], P(('row', 'col'))
The draws below stay inside these ranges and needn't reach their ends.
Inputs may be any that keep to these rules, and one draw needn't show every extreme that they name: `scen_inverse`: each block is full rank and well conditioned. `schur_inverse`: full rank and well conditioned.
All inputs are finite; a program needn't handle non-finite values.
Results may differ from the reference program's by a relative error of at most 0.005.
Values may be sent and summed in bfloat16 or wider, within the bound.
No kernel may reach another device: no remote copies, remote signals or barrier semaphores. Data moves between devices by JAX's collectives and lax.ppermute only.
A program may use at most 128 MiB of HBM per device.

```python
import jax
import jax.numpy as jnp
from jax import lax

M = 512
N = 3072
R = 256
SCEN = 64


def dominant(key, count, order):
    first, second = jax.random.split(key, 2)
    spread = jax.random.truncated_normal(first, -4.0, 4.0, (count, order, order), jnp.float32) * (0.5 / order ** 0.5)
    middle = jax.random.uniform(second, (count, order), jnp.float32, 0.5, 1.5)
    matrix = spread + middle[:, :, None] * jnp.eye(order, dtype=jnp.float32)[None]
    return matrix


def draw_scen_inverse(key, part):
    return dominant(jax.random.fold_in(key, 11), SCEN, M).astype(jnp.bfloat16)


def draw_schur_inverse(key, part):
    return dominant(jax.random.fold_in(key, 23), 1, N)[0]


def raised(result, stream_key, source, target, shards_of, factor):
    def block_of(dim):
        return (jnp.arange(result.shape[dim]) // (result.shape[dim] // shards_of)).reshape((-1,) + (1,) * (result.ndim - 1 - dim))

    first = jax.random.permutation(stream_key, shards_of)[block_of(target)]
    other_side = (block_of(target) + shards_of // 2) % shards_of
    return jnp.where((block_of(source) == first) | (block_of(source) == other_side), factor * result, result)


def levels(own_key, dims, pieces, least, top_value):
    factor_of, own = 1.0, jax.random.fold_in(own_key, 6)
    for axis_at, parts in pieces:
        draws = jnp.exp(jax.random.uniform(jax.random.fold_in(own, axis_at), (parts,), jnp.float32, least / len(pieces), top_value / len(pieces)))
        factor_of = factor_of * jnp.repeat(draws, dims[axis_at] // parts).reshape([-1 if axis == axis_at else 1 for axis in range(len(dims))])
    return factor_of


def bell_draw(rng, extent, deviation, reach, cuts=(), kind=jnp.bfloat16):
    entries = deviation * jax.random.normal(rng, extent, jnp.float32)
    if cuts:
        entries = entries * levels(rng, extent, cuts, -0.22, 0.18)
    return jnp.clip(entries, -reach, reach).astype(kind)


def noise_with(key, shape, deviation, bound, shards, heavy, kind=jnp.bfloat16):
    array = deviation * jax.random.normal(key, shape, jnp.float32)
    if shards:
        array = array * levels(key, shape, shards, -0.22, 0.18)
    return jnp.clip(raised(array, jax.random.fold_in(key, 3), *heavy), -bound, bound).astype(kind)


def setup_inputs(seed: int = 0) -> dict:
    splits = jax.random.split(jax.random.key(seed), 8)
    return {
        "scen_inverse": draw_scen_inverse(jax.random.fold_in(splits[7], 71), 0),
        "coupling": noise_with(splits[1], (SCEN, M, N), (SCEN * M) ** -0.5, 0.0625, ((0, 32),), (0, 2, 32, 2.75)),
        "scen_cot": bell_draw(splits[2], (SCEN, M, R), 1.0, 6.0, ((0, 32),)),
        "first_cot": bell_draw(splits[3], (N, R), 1.0, 6.0, ((0, 4),), jnp.float32),
        "schur_inverse": draw_schur_inverse(jax.random.fold_in(splits[7], 71), 0),
        "scen_primal": bell_draw(splits[5], (SCEN, M, R), R ** -0.5, 0.375, ((0, 32),)),
        "first_primal": bell_draw(splits[6], (N, R), R ** -0.5, 0.375),
    }


def reference(scen_inverse, coupling, scen_cot, first_cot, schur_inverse, scen_primal, first_primal):
    def condense(total, item):
        inverse, couple, cot = item
        helper = jnp.dot(inverse.T, cot, preferred_element_type=jnp.float32).astype(jnp.bfloat16)
        return total + jnp.dot(couple.T, helper, preferred_element_type=jnp.float32), None

    summed, _ = lax.scan(condense, jnp.zeros((N, R), jnp.float32), (scen_inverse, coupling, scen_cot))
    condensed = first_cot - summed
    first_adjoint = jnp.dot(schur_inverse.T, condensed, precision=lax.Precision.HIGHEST, preferred_element_type=jnp.float32)
    adjoint_low = first_adjoint.astype(jnp.bfloat16)

    def recover(item):
        inverse, couple, cot, primal = item
        update = (cot.astype(jnp.float32) - jnp.dot(couple, adjoint_low, preferred_element_type=jnp.float32)).astype(jnp.bfloat16)
        adjoint = jnp.dot(inverse.T, update, preferred_element_type=jnp.float32)
        scen_low = adjoint.astype(jnp.bfloat16)
        gradient = -(jnp.dot(scen_low, first_primal.T, preferred_element_type=jnp.float32) + jnp.dot(primal, adjoint_low.T, preferred_element_type=jnp.float32))
        return adjoint, gradient

    scen_adjoint, coupling_grad = lax.map(recover, (scen_inverse, coupling, scen_cot, scen_primal))
    return scen_adjoint, first_adjoint, coupling_grad
```

```python
import jax
import jax.numpy as jnp
from jax import lax
from jax.sharding import PartitionSpec as P

F32 = jnp.float32
BF16 = jnp.bfloat16


def swap(value, axis, mask):
    size = lax.axis_size(axis)
    return lax.ppermute(value, axis, [(i, i ^ mask) for i in range(size)])


def body(scen_inverse, coupling, scen_cot, first_cot, schur_inverse, scen_primal, first_primal):
    rows, cols = lax.axis_size("row"), lax.axis_size("col")
    row, col = lax.axis_index("row"), lax.axis_index("col")
    core = col % 2
    levels = cols // 2
    level = col // 2
    directions = scen_cot.shape[2]
    half = directions // 2
    depth = first_cot.shape[0]
    width = schur_inverse.shape[1]
    part = directions // rows

    helper = jnp.einsum("smk,smr->srk", scen_inverse, scen_cot, preferred_element_type=F32).astype(BF16)
    term = jnp.einsum("srm,smn->rn", helper, coupling, preferred_element_type=F32)

    low, high = term[:half], term[half:]
    keep = jnp.where(core == 0, low, high)
    give = jnp.where(core == 0, high, low)
    chip = keep + swap(give.astype(BF16), "col", 1).astype(F32)

    def tile(mask):
        return lax.dynamic_slice(chip, (0, (row ^ mask) * depth), (half, depth))

    order = sorted(range(1, rows), key=lambda m: -bin(m).count("1"))
    arrived = [swap(tile(mask).astype(BF16), "row", mask) for mask in order]
    total = tile(0)
    for value in arrived:
        total = total + value.astype(F32)

    mask = 2
    while mask < cols:
        other = mask if 2 * mask < cols else cols - 2
        total = total + swap(total.astype(BF16), "col", other).astype(F32)
        mask *= 2
    cot_t = first_cot.T
    condensed_half = jnp.where(core == 0, cot_t[:half], cot_t[half:]) - total
    sibling = swap(condensed_half, "col", 1)
    condensed = jnp.where(
        core == 0,
        jnp.concatenate([condensed_half, sibling], 0),
        jnp.concatenate([sibling, condensed_half], 0),
    )

    product = jnp.dot(condensed, schur_inverse, precision=lax.Precision.HIGHEST, preferred_element_type=F32)

    def piece(mask):
        return lax.dynamic_slice(product, ((row ^ mask) * part, 0), (part, width))

    arrived = [swap(piece(mask).astype(BF16), "row", mask) for mask in order]
    mine = piece(0)
    for value in arrived:
        mine = mine + value.astype(F32)
    mine = mine.astype(BF16)

    stack = jnp.concatenate([mine] + [swap(mine, "col", 2 * m) for m in range(1, levels)], 0)
    stacks = [stack] + [None] * (rows - 1)
    for mask in order:
        stacks[mask] = swap(stack, "row", mask)
    own = jnp.stack(stacks)
    theirs = swap(own, "col", 1)
    every = jnp.stack([own, theirs]).reshape(2, rows, levels, part, width)

    def ordered(value, axis, index):
        bit = 1
        size = value.shape[axis]
        while bit < size:
            shape = value.shape
            split = value.reshape(shape[:axis] + (size // (2 * bit), 2, bit) + shape[axis + 1 :])
            value = jnp.where((index & bit) != 0, jnp.flip(split, axis + 1), split).reshape(shape)
            bit *= 2
        return value

    every = ordered(every, 0, core)
    every = ordered(every, 1, row)
    every = ordered(every, 2, level)
    adjoint_t = every.transpose(1, 3, 2, 0, 4).reshape(directions, cols * width)
    first_adjoint = lax.dynamic_slice(adjoint_t, (0, col * width), (directions, width)).T.astype(F32)

    update = (
        scen_cot.astype(F32) - jnp.einsum("smn,rn->smr", coupling, adjoint_t, preferred_element_type=F32)
    ).astype(BF16)
    scen_adjoint = jnp.einsum("smk,smr->skr", scen_inverse, update, preferred_element_type=F32)
    scen_low = scen_adjoint.astype(BF16)
    coupling_grad = -(
        jnp.einsum("smr,nr->smn", scen_low, first_primal, preferred_element_type=F32)
        + jnp.einsum("smr,rn->smn", scen_primal, adjoint_t, preferred_element_type=F32)
    )
    return (scen_adjoint, first_adjoint, coupling_grad)


def solution(mesh):
    return jax.shard_map(
        body,
        mesh=mesh,
        in_specs=(
            P(("row", "col"), None, None),
            P(("row", "col"), None, None),
            P(("row", "col"), None, None),
            P("row", None),
            P("row", "col"),
            P(("row", "col"), None, None),
            P(),
        ),
        out_specs=(P(("row", "col"), None, None), P("col", None), P(("row", "col"), None, None)),
        check_vma=False,
    )
```

```python
import functools

import jax
import jax.numpy as jnp
from jax import lax
from jax.experimental import pallas as pl
from jax.experimental.pallas import tpu as pltpu
from jax.sharding import PartitionSpec as P

F32 = jnp.float32
BF16 = jnp.bfloat16
VMEM = pl.BlockSpec(memory_space=pltpu.VMEM)
SMEM = pl.BlockSpec(memory_space=pltpu.SMEM)
ANY = pl.BlockSpec(memory_space=pl.ANY)
LIMIT = 56 * 1024 * 1024


def swap(value, axis, mask):
    size = lax.axis_size(axis)
    return lax.ppermute(value, axis, [(i, i ^ mask) for i in range(size)])


def dot(a, b):
    return jnp.dot(a, b, preferred_element_type=F32)


def dot_nt(a, b):
    return lax.dot_general(a, b, (((1,), (1,)), ((), ())), preferred_element_type=F32)


def dot_tn(a, b):
    return lax.dot_general(a, b, (((0,), (0,)), ((), ())), preferred_element_type=F32)


def condense_kernel(order, place, inverse, cot, coupling, *rest):
    outs, (helper, block, arrived) = rest[: 2 * len(order)], rest[2 * len(order) :]
    row, core = place[0], place[1]
    count, size = cot.shape[:2]
    half, depth = outs[0].shape
    copies = []
    for i, mask in enumerate(order):
        columns = pl.ds(pl.multiple_of((row ^ mask) * depth, 128), depth)
        copies.append(pltpu.make_async_copy(coupling.at[:, :, columns], block.at[i], arrived.at[i]))
        copies[-1].start()
    for s in range(count):
        value = dot_tn(cot[s], inverse[s]).astype(BF16)
        helper[core, :, s * size : (s + 1) * size] = value[:half]
        helper[1 - core, :, s * size : (s + 1) * size] = value[half:]
    left = helper[...].reshape(2 * half, count * size)
    for i in range(len(order)):
        copies[i].wait()
        value = dot(left, block[i].reshape(count * size, depth))
        outs[2 * i][...] = value[:half]
        outs[2 * i + 1][...] = value[half:].astype(BF16)


def condense(order, place, inverse, cot, coupling, depth):
    count, size, directions = cot.shape
    half = directions // 2
    outs = [jax.ShapeDtypeStruct((half, depth), kind) for _ in order for kind in (F32, BF16)]
    flops = 2 * count * size * directions * (size + len(order) * depth)
    return pl.pallas_call(
        functools.partial(condense_kernel, order),
        out_shape=outs,
        in_specs=[SMEM, VMEM, VMEM, ANY],
        out_specs=[VMEM] * len(outs),
        scratch_shapes=[
            pltpu.VMEM((2, half, count * size), BF16),
            pltpu.VMEM((len(order), count, size, depth), BF16),
            pltpu.SemaphoreType.DMA((len(order),)),
        ],
        compiler_params=pltpu.CompilerParams(vmem_limit_bytes=LIMIT),
        cost_estimate=pl.CostEstimate(flops=flops, bytes_accessed=8 << 20, transcendentals=0),
        name="condense",
    )(place, inverse, cot, coupling)


def prepare_kernel(schur, inverse, high, low, turned):
    value = schur[...].T
    top = value.astype(BF16)
    high[...] = top
    low[...] = (value - top.astype(F32)).astype(BF16)
    for s in range(inverse.shape[0]):
        turned[s] = inverse[s].astype(F32).T.astype(BF16)


def prepare(schur, inverse):
    depth, width = schur.shape
    split = jax.ShapeDtypeStruct((width, depth), BF16)
    return pl.pallas_call(
        prepare_kernel,
        out_shape=[split, split, jax.ShapeDtypeStruct(inverse.shape, BF16)],
        in_specs=[VMEM, VMEM],
        out_specs=[VMEM] * 3,
        compiler_params=pltpu.CompilerParams(vmem_limit_bytes=LIMIT),
        cost_estimate=pl.CostEstimate(flops=1 << 20, bytes_accessed=8 << 20, transcendentals=0),
        name="prepare",
    )(schur, inverse)


def product_kernel(masks, place, cot, total, last, high, low, high2, low2, *rest):
    outs, value = rest[:-1], rest[-1]
    row, core = place[0], place[1]
    width = high.shape[0]
    part = outs[0].shape[0]
    right = cot[...] - (total[...] + last[...].astype(F32))
    top = right.astype(BF16)
    rest_ = (right - top.astype(F32)).astype(BF16)
    for at, (a, b) in ((core, (high, low)), (1 - core, (high2, low2))):
        part_sum = dot_nt(a[...], top) + dot_nt(a[...], rest_) + dot_nt(b[...], top)
        value[pl.ds(pl.multiple_of(at * width, 16), width), :] = part_sum
    for mask, out in zip(masks, outs):
        piece = value[pl.ds(pl.multiple_of((row ^ mask) * part, 16), part), :]
        out[...] = piece.astype(out.dtype)


def product(masks, place, cot, total, last, high, low, high2, low2):
    half, depth = cot.shape
    width = high.shape[0]
    part = 2 * width // len(masks)
    outs = [jax.ShapeDtypeStruct((part, half), BF16 if mask else F32) for mask in masks]
    return pl.pallas_call(
        functools.partial(product_kernel, masks),
        out_shape=outs,
        in_specs=[SMEM] + [VMEM] * 7,
        out_specs=[VMEM] * len(outs),
        scratch_shapes=[pltpu.VMEM((2 * width, half), F32)],
        compiler_params=pltpu.CompilerParams(vmem_limit_bytes=LIMIT),
        cost_estimate=pl.CostEstimate(flops=12 * width * depth * half, bytes_accessed=4 << 20, transcendentals=0),
        name="product",
    )(place, cot, total, last, high, low, high2, low2)


def recover_kernel(rows, place, coupling, cot, turned, primal, first_primal, *rest):
    stacks = rest[: 2 * rows]
    scen_adjoint, first_adjoint, grad, adjoint, couple, update, tile, arrived, left = rest[2 * rows :]
    row, core, level = place[0], place[1], place[2]
    count, size, total = couple.shape
    half = stacks[0].shape[1]
    width = first_adjoint.shape[0]
    part = 2 * width // rows
    levels = stacks[0].shape[0] // part
    loads = [pltpu.make_async_copy(coupling.at[s], couple.at[s], arrived.at[s]) for s in range(count)]
    for load in loads:
        load.start()
    for side in range(2):
        lanes = pl.ds(pl.multiple_of((core ^ side) * half, 128), half)
        for mask in range(rows):
            for step in range(levels):
                start = (level ^ step) * (2 * width) + (row ^ mask) * part
                piece = stacks[side * rows + mask][step * part : (step + 1) * part, :]
                adjoint[pl.ds(pl.multiple_of(start, 16), part), lanes] = piece
    start = pl.multiple_of((level * 2 + core) * width, 16)
    first_adjoint[...] = adjoint[pl.ds(start, width), :].astype(F32)
    chunk = total // rows
    stores = []
    for s in range(count):
        loads[s].wait()
        value = dot(couple[s], adjoint[...])
        update[...] = (cot[s].astype(F32) - value).astype(BF16)
        value = dot(turned[s], update[...])
        scen_adjoint[s] = value
        low = value.astype(BF16)
        for i in range(rows):
            columns = slice(i * chunk, (i + 1) * chunk)
            slot = s * rows + i
            tile[slot] = -(dot_nt(low, first_primal[columns, :]) + dot_nt(primal[s], adjoint[columns, :]))
            stores.append(pltpu.make_async_copy(tile.at[slot], grad.at[s, :, pl.ds(i * chunk, chunk)], left.at[slot]))
            stores[-1].start()
    for store in stores:
        store.wait()


def recover(rows, place, coupling, cot, turned, primal, first_primal, stacks, width):
    count, size, total = coupling.shape
    directions = cot.shape[2]
    chunk = total // rows
    outs = [
        jax.ShapeDtypeStruct(cot.shape, F32),
        jax.ShapeDtypeStruct((width, directions), F32),
        jax.ShapeDtypeStruct(coupling.shape, F32),
    ]
    return pl.pallas_call(
        functools.partial(recover_kernel, rows),
        out_shape=outs,
        in_specs=[SMEM, ANY] + [VMEM] * (4 + len(stacks)),
        out_specs=[VMEM, VMEM, ANY],
        scratch_shapes=[
            pltpu.VMEM((total, directions), BF16),
            pltpu.VMEM((count, size, total), BF16),
            pltpu.VMEM((size, directions), BF16),
            pltpu.VMEM((count * rows, size, chunk), F32),
            pltpu.SemaphoreType.DMA((count,)),
            pltpu.SemaphoreType.DMA((count * rows,)),
        ],
        compiler_params=pltpu.CompilerParams(vmem_limit_bytes=LIMIT),
        cost_estimate=pl.CostEstimate(
            flops=2 * count * size * directions * (3 * total + size), bytes_accessed=24 << 20, transcendentals=0
        ),
        name="recover",
    )(place, coupling, cot, turned, primal, first_primal, *stacks)


def body(scen_inverse, coupling, scen_cot, first_cot, schur_inverse, scen_primal, first_primal):
    rows, cols = lax.axis_size("row"), lax.axis_size("col")
    row, col = lax.axis_index("row"), lax.axis_index("col")
    core, level, levels = col % 2, col // 2, cols // 2
    place = jnp.stack([row, core, level]).astype(jnp.int32)
    half = scen_cot.shape[2] // 2
    depth, width = schur_inverse.shape
    far = sorted(range(1, rows), key=lambda m: -bin(m).count("1"))

    terms = condense(far + [0], place, scen_inverse, scen_cot, coupling, depth)
    chips = [keep + swap(give, "col", 1).astype(F32) for keep, give in zip(terms[0::2], terms[1::2])]

    arrived = [swap(chip.astype(BF16), "row", mask) for mask, chip in zip(far, chips)]
    total = chips[-1]
    for value in arrived:
        total = total + value.astype(F32)

    high, low, turned = prepare(schur_inverse, scen_inverse)
    high2, low2 = swap(high, "col", 1), swap(low, "col", 1)
    cot_half = lax.dynamic_slice(first_cot, (0, core * half), (depth, half)).T

    mask = 2
    last = None
    while mask < cols:
        if last is not None:
            total = total + last.astype(F32)
        last = swap(total.astype(BF16), "col", mask if 2 * mask < cols else cols - 2)
        mask *= 2

    pieces = product([0] + far, place, cot_half, total, last, high, low, high2, low2)
    mine = pieces[0]
    for mask, piece in zip(far, pieces[1:]):
        mine = mine + swap(piece, "row", mask).astype(F32)
    mine = mine.astype(BF16)

    stack = jnp.concatenate([mine] + [swap(mine, "col", 2 * m) for m in range(1, levels)], 0)
    stacks = [stack] + [None] * (rows - 1)
    for mask in far:
        stacks[mask] = swap(stack, "row", mask)
    stacks = stacks + [swap(value, "col", 1) for value in stacks]
    scen_adjoint, first_adjoint, coupling_grad = recover(
        rows, place, coupling, scen_cot, turned, scen_primal, first_primal, stacks, width
    )
    return (scen_adjoint, first_adjoint, coupling_grad)


def solution(mesh):
    return jax.shard_map(
        body,
        mesh=mesh,
        in_specs=(
            P(("row", "col"), None, None),
            P(("row", "col"), None, None),
            P(("row", "col"), None, None),
            P("row", None),
            P("row", "col"),
            P(("row", "col"), None, None),
            P(),
        ),
        out_specs=(P(("row", "col"), None, None), P("col", None), P(("row", "col"), None, None)),
        check_vma=False,
    )
```

```python
import functools

import jax
import jax.numpy as jnp
from jax import lax
from jax.experimental import pallas as pl
from jax.experimental.pallas import tpu as pltpu
from jax.sharding import PartitionSpec as P

F32 = jnp.float32
BF16 = jnp.bfloat16
VMEM = pl.BlockSpec(memory_space=pltpu.VMEM)
SMEM = pl.BlockSpec(memory_space=pltpu.SMEM)
ANY = pl.BlockSpec(memory_space=pl.ANY)
MIB = 1024 * 1024


def swap(value, axis, mask):
    size = lax.axis_size(axis)
    return lax.ppermute(value, axis, [(i, i ^ mask) for i in range(size)])


def dot(a, b):
    return jnp.dot(a, b, preferred_element_type=F32)


def dot_nt(a, b):
    return lax.dot_general(a, b, (((1,), (1,)), ((), ())), preferred_element_type=F32)


def dot_tn(a, b):
    return lax.dot_general(a, b, (((0,), (0,)), ((), ())), preferred_element_type=F32)


def condense_kernel(order, place, inverse, cot, coupling, *rest):
    outs, (helper, own_inverse, own_cot, block, arrived) = rest[: 2 * len(order)], rest[2 * len(order) :]
    row, core = place[0], place[1]
    count, size = cot.shape[:2]
    half, depth = outs[0].shape
    copies = [
        pltpu.make_async_copy(cot, own_cot, arrived.at[0]),
        pltpu.make_async_copy(inverse, own_inverse, arrived.at[1]),
    ]
    for i, mask in enumerate(order):
        columns = pl.ds(pl.multiple_of((row ^ mask) * depth, 128), depth)
        copies.append(pltpu.make_async_copy(coupling.at[:, :, columns], block.at[i], arrived.at[2 + i]))
    for copy in copies:
        copy.start()
    copies[0].wait()
    copies[1].wait()
    for s in range(count):
        value = dot_tn(own_cot[s], own_inverse[s]).astype(BF16)
        helper[core, :, s * size : (s + 1) * size] = value[:half]
        helper[1 - core, :, s * size : (s + 1) * size] = value[half:]
    left = helper[...].reshape(2 * half, count * size)
    for i in range(len(order)):
        copies[2 + i].wait()
        value = dot(left, block[i].reshape(count * size, depth))
        outs[2 * i][...] = value[:half]
        outs[2 * i + 1][...] = value[half:].astype(BF16)


def condense(order, place, inverse, cot, coupling, depth):
    count, size, directions = cot.shape
    half = directions // 2
    outs = [pltpu.VMEM((half, depth), kind) for _ in order for kind in (F32, BF16)]
    flops = 2 * count * size * directions * (size + len(order) * depth)
    inputs = [pltpu.with_memory_space_constraint(value, pltpu.HBM) for value in (inverse, cot, coupling)]
    return pl.pallas_call(
        functools.partial(condense_kernel, order),
        out_shape=outs,
        in_specs=[SMEM, ANY, ANY, ANY],
        out_specs=[VMEM] * len(outs),
        scratch_shapes=[
            pltpu.VMEM((2, half, count * size), BF16),
            pltpu.VMEM(inverse.shape, BF16),
            pltpu.VMEM(cot.shape, BF16),
            pltpu.VMEM((len(order), count, size, depth), BF16),
            pltpu.SemaphoreType.DMA((2 + len(order),)),
        ],
        compiler_params=pltpu.CompilerParams(vmem_limit_bytes=20 * MIB),
        cost_estimate=pl.CostEstimate(flops=flops, bytes_accessed=8 << 20, transcendentals=0),
        name="condense",
    )(place, *inputs)


def prepare_kernel(schur, inverse, high, low, turned):
    value = schur[...].T
    top = value.astype(BF16)
    high[...] = top
    low[...] = (value - top.astype(F32)).astype(BF16)
    for s in range(inverse.shape[0]):
        turned[s] = inverse[s].astype(F32).T.astype(BF16)


def prepare(schur, inverse):
    depth, width = schur.shape
    split = jax.ShapeDtypeStruct((width, depth), BF16)
    return pl.pallas_call(
        prepare_kernel,
        out_shape=[split, split, jax.ShapeDtypeStruct(inverse.shape, BF16)],
        in_specs=[VMEM, VMEM],
        out_specs=[VMEM] * 3,
        compiler_params=pltpu.CompilerParams(vmem_limit_bytes=12 * MIB),
        cost_estimate=pl.CostEstimate(flops=1 << 20, bytes_accessed=8 << 20, transcendentals=0),
        name="prepare",
    )(schur, inverse)


def product_kernel(masks, place, cot, total, last, high, low, high2, low2, *rest):
    outs, value = rest[:-1], rest[-1]
    row, core = place[0], place[1]
    width = high.shape[0]
    part = outs[0].shape[0]
    right = cot[...] - (total[...] + last[...].astype(F32))
    top = right.astype(BF16)
    rest_ = (right - top.astype(F32)).astype(BF16)
    for at, (a, b) in ((core, (high, low)), (1 - core, (high2, low2))):
        part_sum = dot_nt(a[...], top) + dot_nt(a[...], rest_) + dot_nt(b[...], top)
        value[pl.ds(pl.multiple_of(at * width, 16), width), :] = part_sum
    for mask, out in zip(masks, outs):
        piece = value[pl.ds(pl.multiple_of((row ^ mask) * part, 16), part), :]
        out[...] = piece.astype(out.dtype)


def product(masks, place, cot, total, last, high, low, high2, low2):
    half, depth = cot.shape
    width = high.shape[0]
    part = 2 * width // len(masks)
    outs = [pltpu.VMEM((part, half), BF16 if mask else F32) for mask in masks]
    return pl.pallas_call(
        functools.partial(product_kernel, masks),
        out_shape=outs,
        in_specs=[SMEM] + [VMEM] * 7,
        out_specs=[VMEM] * len(outs),
        scratch_shapes=[pltpu.VMEM((2 * width, half), F32)],
        compiler_params=pltpu.CompilerParams(vmem_limit_bytes=12 * MIB),
        cost_estimate=pl.CostEstimate(flops=12 * width * depth * half, bytes_accessed=4 << 20, transcendentals=0),
        name="product",
    )(place, cot, total, last, high, low, high2, low2)


def recover_kernel(rows, place, coupling, cot, turned, primal, first_primal, *rest):
    stacks = rest[: 2 * rows]
    scen_adjoint, first_adjoint, grad, adjoint, update, tile, left = rest[2 * rows :]
    row, core, level = place[0], place[1], place[2]
    count, size, total = coupling.shape
    half = stacks[0].shape[1]
    width = first_adjoint.shape[0]
    part = 2 * width // rows
    levels = stacks[0].shape[0] // part
    for side in range(2):
        lanes = pl.ds(pl.multiple_of((core ^ side) * half, 128), half)
        for mask in range(rows):
            for step in range(levels):
                start = (level ^ step) * (2 * width) + (row ^ mask) * part
                piece = stacks[side * rows + mask][step * part : (step + 1) * part, :]
                adjoint[pl.ds(pl.multiple_of(start, 16), part), lanes] = piece
    start = pl.multiple_of((level * 2 + core) * width, 16)
    first_adjoint[...] = adjoint[pl.ds(start, width), :].astype(F32)
    chunk = total // rows
    stores = []
    for s in range(count):
        value = dot(coupling[s], adjoint[...])
        update[...] = (cot[s].astype(F32) - value).astype(BF16)
        value = dot(turned[s], update[...])
        scen_adjoint[s] = value
        low = value.astype(BF16)
        for i in range(rows):
            columns = slice(i * chunk, (i + 1) * chunk)
            slot = s * rows + i
            tile[slot] = -(dot_nt(low, first_primal[columns, :]) + dot_nt(primal[s], adjoint[columns, :]))
            stores.append(pltpu.make_async_copy(tile.at[slot], grad.at[s, :, pl.ds(i * chunk, chunk)], left.at[slot]))
            stores[-1].start()
    for store in stores:
        store.wait()


def recover(rows, place, coupling, cot, turned, primal, first_primal, stacks, width):
    count, size, total = coupling.shape
    directions = cot.shape[2]
    chunk = total // rows
    outs = [
        jax.ShapeDtypeStruct(cot.shape, F32),
        jax.ShapeDtypeStruct((width, directions), F32),
        jax.ShapeDtypeStruct(coupling.shape, F32),
    ]
    return pl.pallas_call(
        functools.partial(recover_kernel, rows),
        out_shape=outs,
        in_specs=[SMEM] + [VMEM] * (5 + len(stacks)),
        out_specs=[VMEM, VMEM, ANY],
        scratch_shapes=[
            pltpu.VMEM((total, directions), BF16),
            pltpu.VMEM((size, directions), BF16),
            pltpu.VMEM((count * rows, size, chunk), F32),
            pltpu.SemaphoreType.DMA((count * rows,)),
        ],
        compiler_params=pltpu.CompilerParams(vmem_limit_bytes=24 * MIB),
        cost_estimate=pl.CostEstimate(
            flops=2 * count * size * directions * (3 * total + size), bytes_accessed=24 << 20, transcendentals=0
        ),
        name="recover",
    )(place, coupling, cot, turned, primal, first_primal, *stacks)


def body(scen_inverse, coupling, scen_cot, first_cot, schur_inverse, scen_primal, first_primal):
    rows, cols = lax.axis_size("row"), lax.axis_size("col")
    row, col = lax.axis_index("row"), lax.axis_index("col")
    core, level, levels = col % 2, col // 2, cols // 2
    place = jnp.stack([row, core, level]).astype(jnp.int32)
    half = scen_cot.shape[2] // 2
    depth, width = schur_inverse.shape
    far = sorted(range(1, rows), key=lambda m: -bin(m).count("1"))

    terms = condense(far + [0], place, scen_inverse, scen_cot, coupling, depth)
    chips = [keep + swap(give, "col", 1).astype(F32) for keep, give in zip(terms[0::2], terms[1::2])]

    arrived = [swap(chip.astype(BF16), "row", mask) for mask, chip in zip(far, chips)]
    total = chips[-1]
    for value in arrived:
        total = total + value.astype(F32)

    high, low, turned = prepare(schur_inverse, scen_inverse)
    total, high, low, turned = lax.optimization_barrier((total, high, low, turned))
    high2, low2 = swap(high, "col", 1), swap(low, "col", 1)
    cot_half = lax.dynamic_slice(first_cot, (0, core * half), (depth, half)).T

    mask = 2
    last = None
    while mask < cols:
        if last is not None:
            total = total + last.astype(F32)
        last = swap(total.astype(BF16), "col", mask if 2 * mask < cols else cols - 2)
        mask *= 2

    pieces = product([0] + far, place, cot_half, total, last, high, low, high2, low2)
    mine = pieces[0]
    for mask, piece in zip(far, pieces[1:]):
        mine = mine + swap(piece, "row", mask).astype(F32)
    mine = mine.astype(BF16)

    stack = jnp.concatenate([mine] + [swap(mine, "col", 2 * m) for m in range(1, levels)], 0)
    stacks = [stack] + [None] * (rows - 1)
    for mask in far:
        stacks[mask] = swap(stack, "row", mask)
    stacks = stacks + [swap(value, "col", 1) for value in stacks]
    scen_adjoint, first_adjoint, coupling_grad = recover(
        rows, place, coupling, scen_cot, turned, scen_primal, first_primal, stacks, width
    )
    return (scen_adjoint, first_adjoint, coupling_grad)


def solution(mesh):
    return jax.shard_map(
        body,
        mesh=mesh,
        in_specs=(
            P(("row", "col"), None, None),
            P(("row", "col"), None, None),
            P(("row", "col"), None, None),
            P("row", None),
            P("row", "col"),
            P(("row", "col"), None, None),
            P(),
        ),
        out_specs=(P(("row", "col"), None, None), P("col", None), P(("row", "col"), None, None)),
        check_vma=False,
    )
```

```python
import functools

import jax
import jax.numpy as jnp
from jax import lax
from jax.experimental import pallas as pl
from jax.experimental.pallas import tpu as pltpu
from jax.sharding import PartitionSpec as P

F32 = jnp.float32
BF16 = jnp.bfloat16
VMEM = pl.BlockSpec(memory_space=pltpu.VMEM)
SMEM = pl.BlockSpec(memory_space=pltpu.SMEM)
ANY = pl.BlockSpec(memory_space=pl.ANY)
MIB = 1024 * 1024


def swap(value, axis, mask):
    size = lax.axis_size(axis)
    return lax.ppermute(value, axis, [(i, i ^ mask) for i in range(size)])


def dot(a, b):
    return jnp.dot(a, b, preferred_element_type=F32)


def dot_nt(a, b):
    return lax.dot_general(a, b, (((1,), (1,)), ((), ())), preferred_element_type=F32)


def dot_tn(a, b):
    return lax.dot_general(a, b, (((0,), (0,)), ((), ())), preferred_element_type=F32)


def condense_kernel(mask, first, place, *refs):
    row, core = place[0], place[1]
    if first:
        inverse, cot, coupling, keep, give, block, helper, own_inverse, own_cot, arrived = refs
    else:
        helper, coupling, keep, give, block, arrived = refs
    count, size, depth = block.shape
    half = keep.shape[0]
    columns = pl.ds(pl.multiple_of((row ^ mask) * depth, 128), depth)
    last = pltpu.make_async_copy(coupling.at[:, :, columns], block, arrived.at[0])
    if first:
        copies = [
            pltpu.make_async_copy(cot, own_cot, arrived.at[1]),
            pltpu.make_async_copy(inverse, own_inverse, arrived.at[2]),
        ]
        for copy in copies:
            copy.start()
        last.start()
        for copy in copies:
            copy.wait()
        for s in range(count):
            value = dot_tn(own_cot[s], own_inverse[s]).astype(BF16)
            helper[core, :, s * size : (s + 1) * size] = value[:half]
            helper[1 - core, :, s * size : (s + 1) * size] = value[half:]
    else:
        last.start()
    left = helper[...].reshape(2 * half, count * size)
    last.wait()
    value = dot(left, block[...].reshape(count * size, depth))
    keep[...] = value[:half]
    give[...] = value[half:].astype(BF16)


def condense(mask, place, inverse, cot, coupling, helper, depth):
    count, size, directions = cot.shape
    half = directions // 2
    first = helper is None
    outs = [pltpu.VMEM((half, depth), F32), pltpu.VMEM((half, depth), BF16), pltpu.VMEM((count, size, depth), BF16)]
    inputs = [inverse, cot, coupling] if first else [coupling]
    inputs = [pltpu.with_memory_space_constraint(value, pltpu.HBM) for value in inputs]
    specs = [ANY] * len(inputs)
    if first:
        outs += [pltpu.VMEM((2, half, count * size), BF16)]
        outs += [pltpu.VMEM(inverse.shape, BF16), pltpu.VMEM(cot.shape, BF16)]
    else:
        inputs, specs = [helper] + inputs, [VMEM] + specs
    return pl.pallas_call(
        functools.partial(condense_kernel, mask, first),
        out_shape=outs,
        in_specs=[SMEM] + specs,
        out_specs=[VMEM] * len(outs),
        scratch_shapes=[pltpu.SemaphoreType.DMA((3,))],
        compiler_params=pltpu.CompilerParams(vmem_limit_bytes=12 * MIB),
        cost_estimate=pl.CostEstimate(
            flops=2 * count * size * directions * depth, bytes_accessed=2 << 20, transcendentals=0
        ),
        name="condense",
    )(place, *inputs)


def prepare_kernel(place, schur, inverse, first_cot, high, low, turned, cot_half):
    half = cot_half.shape[0]
    value = schur[...].T
    top = value.astype(BF16)
    high[...] = top
    low[...] = (value - top.astype(F32)).astype(BF16)
    for s in range(inverse.shape[0]):
        turned[s] = inverse[s].astype(F32).T.astype(BF16)
    cot_half[...] = first_cot[:, pl.ds(pl.multiple_of(place[1] * half, 128), half)].T


def prepare(place, schur, inverse, first_cot):
    depth, width = schur.shape
    split = pltpu.VMEM((width, depth), BF16)
    return pl.pallas_call(
        prepare_kernel,
        out_shape=[
            split,
            split,
            pltpu.VMEM(inverse.shape, BF16),
            pltpu.VMEM((first_cot.shape[1] // 2, depth), F32),
        ],
        in_specs=[SMEM, VMEM, VMEM, VMEM],
        out_specs=[VMEM] * 4,
        compiler_params=pltpu.CompilerParams(vmem_limit_bytes=12 * MIB),
        cost_estimate=pl.CostEstimate(flops=1 << 20, bytes_accessed=4 << 20, transcendentals=0),
        name="prepare",
    )(place, schur, inverse, first_cot)


def product_kernel(masks, place, cot, total, last, high, low, high2, low2, *rest):
    outs, value = rest[:-1], rest[-1]
    row, core = place[0], place[1]
    width = high.shape[0]
    part = outs[0].shape[0]
    right = cot[...] - (total[...] + last[...].astype(F32))
    top = right.astype(BF16)
    rest_ = (right - top.astype(F32)).astype(BF16)
    for at, (a, b) in ((core, (high, low)), (1 - core, (high2, low2))):
        part_sum = dot_nt(a[...], top) + dot_nt(a[...], rest_) + dot_nt(b[...], top)
        value[pl.ds(pl.multiple_of(at * width, 16), width), :] = part_sum
    for mask, out in zip(masks, outs):
        piece = value[pl.ds(pl.multiple_of((row ^ mask) * part, 16), part), :]
        out[...] = piece.astype(out.dtype)


def product(masks, place, cot, total, last, high, low, high2, low2):
    half, depth = cot.shape
    width = high.shape[0]
    part = 2 * width // len(masks)
    outs = [pltpu.VMEM((part, half), BF16 if mask else F32) for mask in masks]
    return pl.pallas_call(
        functools.partial(product_kernel, masks),
        out_shape=outs,
        in_specs=[SMEM] + [VMEM] * 7,
        out_specs=[VMEM] * len(outs),
        scratch_shapes=[pltpu.VMEM((2 * width, half), F32)],
        compiler_params=pltpu.CompilerParams(vmem_limit_bytes=12 * MIB),
        cost_estimate=pl.CostEstimate(flops=12 * width * depth * half, bytes_accessed=4 << 20, transcendentals=0),
        name="product",
    )(place, cot, total, last, high, low, high2, low2)


def recover_kernel(rows, place, first_primal, primal, cot, turned, *rest):
    blocks, stacks, rest = rest[:rows], rest[rows : 3 * rows], rest[3 * rows :]
    scen_adjoint, first_adjoint, grad, right, left, primals, update, adjoints, firsts, tile, arrived, gone = rest
    row, core, level = place[0], place[1], place[2]
    count, size, depth = blocks[0].shape
    total, directions = first_primal.shape
    half = directions // 2
    width = first_adjoint.shape[0]
    part = 2 * width // rows
    levels = stacks[0].shape[0] // part
    loads = [
        pltpu.make_async_copy(first_primal, right.at[:, pl.ds(0, directions)], arrived.at[0]),
        pltpu.make_async_copy(primal, primals, arrived.at[1]),
    ]
    for load in loads:
        load.start()
    for side in range(2):
        lanes = pl.ds(pl.multiple_of(directions + (core ^ side) * half, 128), half)
        for mask in range(rows):
            for step in range(levels):
                start = (level ^ step) * (2 * width) + (row ^ mask) * part
                piece = stacks[side * rows + mask][step * part : (step + 1) * part, :]
                right[pl.ds(pl.multiple_of(start, 16), part), lanes] = piece
    stores = []

    def store(source, target):
        stores.append(pltpu.make_async_copy(source, target, gone.at[len(stores)]))
        stores[-1].start()

    start = pl.multiple_of((level * 2 + core) * width, 16)
    firsts[...] = right[pl.ds(start, width), directions:].astype(F32)
    store(firsts, first_adjoint)
    for s in range(count):
        value = cot[s].astype(F32)
        for mask in range(rows):
            start = pl.multiple_of((row ^ mask) * depth, 128)
            value = value - dot(blocks[mask][s], right[pl.ds(start, depth), directions:])
        update[...] = value.astype(BF16)
        value = dot(turned[s], update[...])
        adjoints[s] = value
        store(adjoints.at[s], scen_adjoint.at[s])
        left[:, :directions] = -value.astype(BF16)
        if s == 0:
            for load in loads:
                load.wait()
        left[:, directions:] = -primals[s]
        for i in range(rows):
            slot = s * rows + i
            tile[slot] = dot_nt(left[...], right[i * depth : (i + 1) * depth, :])
            store(tile.at[slot], grad.at[s, :, pl.ds(i * depth, depth)])
    for copy in stores:
        copy.wait()


def recover(rows, place, first_primal, primal, cot, turned, blocks, stacks, width):
    count, size, depth = blocks[0].shape
    total, directions = first_primal.shape
    outs = [
        jax.ShapeDtypeStruct(cot.shape, F32),
        jax.ShapeDtypeStruct((width, directions), F32),
        jax.ShapeDtypeStruct((count, size, total), F32),
    ]
    inputs = [pltpu.with_memory_space_constraint(value, pltpu.HBM) for value in (first_primal, primal)]
    return pl.pallas_call(
        functools.partial(recover_kernel, rows),
        out_shape=outs,
        in_specs=[SMEM, ANY, ANY] + [VMEM] * (2 + len(blocks) + len(stacks)),
        out_specs=[ANY, ANY, ANY],
        scratch_shapes=[
            pltpu.VMEM((total, 2 * directions), BF16),
            pltpu.VMEM((size, 2 * directions), BF16),
            pltpu.VMEM(primal.shape, BF16),
            pltpu.VMEM((size, directions), BF16),
            pltpu.VMEM(cot.shape, F32),
            pltpu.VMEM((width, directions), F32),
            pltpu.VMEM((count * rows, size, depth), F32),
            pltpu.SemaphoreType.DMA((2,)),
            pltpu.SemaphoreType.DMA((1 + count * (1 + rows),)),
        ],
        compiler_params=pltpu.CompilerParams(vmem_limit_bytes=28 * MIB),
        cost_estimate=pl.CostEstimate(
            flops=2 * count * size * directions * (3 * total + size), bytes_accessed=20 << 20, transcendentals=0
        ),
        name="recover",
    )(place, *inputs, cot, turned, *blocks, *stacks)


def body(scen_inverse, coupling, scen_cot, first_cot, schur_inverse, scen_primal, first_primal):
    rows, cols = lax.axis_size("row"), lax.axis_size("col")
    row, col = lax.axis_index("row"), lax.axis_index("col")
    core, level, levels = col % 2, col // 2, cols // 2
    place = jnp.stack([row, core, level]).astype(jnp.int32)
    half = scen_cot.shape[2] // 2
    depth, width = schur_inverse.shape
    far = sorted(range(1, rows), key=lambda m: -bin(m).count("1"))

    blocks, arrived, ready, helper = [None] * rows, [], [], None
    order = far + [0]

    def send():
        arrived.append(swap(ready[len(arrived)], "row", order[len(arrived)]))

    for i, mask in enumerate(order):
        if i >= 2:
            helper, ready[i - 2] = lax.optimization_barrier((helper, ready[i - 2]))
            send()
        keep, give, blocks[mask], *others = condense(mask, place, scen_inverse, scen_cot, coupling, helper, depth)
        if others:
            helper, own_inverse, own_cot = others
        total = keep + swap(give, "col", 1).astype(F32)
        ready.append(total.astype(BF16))
    while len(arrived) < len(far):
        send()
    for value in arrived:
        total = total + value.astype(F32)

    high, low, turned, cot_half = prepare(place, schur_inverse, own_inverse, first_cot)
    total, high, low, turned, cot_half = lax.optimization_barrier((total, high, low, turned, cot_half))
    high2, low2 = swap(high, "col", 1), swap(low, "col", 1)

    mask = 2
    last = None
    while mask < cols:
        if last is not None:
            total = total + last.astype(F32)
        last = swap(total.astype(BF16), "col", mask if 2 * mask < cols else cols - 2)
        mask *= 2

    pieces = product([0] + far, place, cot_half, total, last, high, low, high2, low2)
    mine = pieces[0]
    for mask, piece in zip(far, pieces[1:]):
        mine = mine + swap(piece, "row", mask).astype(F32)
    mine = mine.astype(BF16)

    stack = jnp.concatenate([mine] + [swap(mine, "col", 2 * m) for m in range(1, levels)], 0)
    stacks = [stack] + [None] * (rows - 1)
    for mask in far:
        stacks[mask] = swap(stack, "row", mask)
    stacks = stacks + [swap(value, "col", 1) for value in stacks]
    scen_adjoint, first_adjoint, coupling_grad = recover(
        rows, place, first_primal, scen_primal, own_cot, turned, blocks, stacks, width
    )
    return (scen_adjoint, first_adjoint, coupling_grad)


def solution(mesh):
    return jax.shard_map(
        body,
        mesh=mesh,
        in_specs=(
            P(("row", "col"), None, None),
            P(("row", "col"), None, None),
            P(("row", "col"), None, None),
            P("row", None),
            P("row", "col"),
            P(("row", "col"), None, None),
            P(),
        ),
        out_specs=(P(("row", "col"), None, None), P("col", None), P(("row", "col"), None, None)),
        check_vma=False,
    )
```

```python
import functools

import jax
import jax.numpy as jnp
from jax import lax
from jax.experimental import pallas as pl
from jax.experimental.pallas import tpu as pltpu
from jax.sharding import PartitionSpec as P

F32 = jnp.float32
BF16 = jnp.bfloat16
VMEM = pl.BlockSpec(memory_space=pltpu.VMEM)
ANY = pl.BlockSpec(memory_space=pl.ANY)
MIB = 1024 * 1024


def swap(value, axis, mask):
    size = lax.axis_size(axis)
    return lax.ppermute(value, axis, [(i, i ^ mask) for i in range(size)])


def place():
    col = lax.axis_index("col")
    return lax.axis_index("row"), lax.rem(col, 2), lax.div(col, 2)


def dot(a, b):
    return jnp.dot(a, b, preferred_element_type=F32)


def dot_nt(a, b):
    return lax.dot_general(a, b, (((1,), (1,)), ((), ())), preferred_element_type=F32)


def dot_tn(a, b):
    return lax.dot_general(a, b, (((0,), (0,)), ((), ())), preferred_element_type=F32)


def condense_kernel(masks, first, *refs):
    row, core, _ = place()
    if first:
        inverse, cot, coupling, *refs = refs
        *outs, helper, own_inverse, own_cot, arrived = refs
    else:
        helper, coupling, *refs = refs
        *outs, arrived = refs
    keeps, gives, blocks = outs[0::3], outs[1::3], outs[2::3]
    count, size, depth = blocks[0].shape
    half = keeps[0].shape[0]
    copies = []
    if first:
        copies.append(pltpu.make_async_copy(cot, own_cot, arrived.at[0]))
        copies.append(pltpu.make_async_copy(inverse, own_inverse, arrived.at[1]))
    for i, mask in enumerate(masks):
        columns = pl.ds(pl.multiple_of((row ^ mask) * depth, 128), depth)
        copies.append(pltpu.make_async_copy(coupling.at[:, :, columns], blocks[i], arrived.at[2 + i]))
    for copy in copies:
        copy.start()
    if first:
        copies.pop(0).wait()
        copies.pop(0).wait()
        for s in range(count):
            value = dot_tn(own_cot[s], own_inverse[s]).astype(BF16)
            helper[core, :, s * size : (s + 1) * size] = value[:half]
            helper[1 - core, :, s * size : (s + 1) * size] = value[half:]
    left = helper[...].reshape(2 * half, count * size)
    for copy, keep, give, block in zip(copies, keeps, gives, blocks):
        copy.wait()
        value = dot(left, block[...].reshape(count * size, depth))
        keep[...] = value[:half]
        give[...] = value[half:].astype(BF16)


def condense(masks, inverse, cot, coupling, helper, depth):
    count, size, directions = cot.shape
    half = directions // 2
    first = helper is None
    outs = [pltpu.VMEM((half, depth), F32), pltpu.VMEM((half, depth), BF16), pltpu.VMEM((count, size, depth), BF16)]
    outs = outs * len(masks)
    inputs = [inverse, cot, coupling] if first else [coupling]
    inputs = [pltpu.with_memory_space_constraint(value, pltpu.HBM) for value in inputs]
    specs = [ANY] * len(inputs)
    if first:
        outs += [pltpu.VMEM((2, half, count * size), BF16)]
        outs += [pltpu.VMEM(inverse.shape, BF16), pltpu.VMEM(cot.shape, BF16)]
    else:
        inputs, specs = [helper] + inputs, [VMEM] + specs
    return pl.pallas_call(
        functools.partial(condense_kernel, masks, first),
        out_shape=outs,
        in_specs=specs,
        out_specs=[VMEM] * len(outs),
        scratch_shapes=[pltpu.SemaphoreType.DMA((2 + len(masks),))],
        compiler_params=pltpu.CompilerParams(vmem_limit_bytes=16 * MIB),
        cost_estimate=pl.CostEstimate(
            flops=2 * count * size * directions * depth * len(masks) if masks != [0] else 1024,
            bytes_accessed=(2 * len(masks)) << 20 if masks != [0] else 1024,
            transcendentals=0,
        ),
        name="condense",
    )(*inputs)


def prepare_kernel(schur, inverse, first_cot, high, low, turned, cot_half):
    half = cot_half.shape[0]
    value = schur[...].T
    top = value.astype(BF16)
    high[...] = top
    low[...] = (value - top.astype(F32)).astype(BF16)
    for s in range(inverse.shape[0]):
        turned[s] = inverse[s].astype(F32).T.astype(BF16)
    cot_half[...] = first_cot[:, pl.ds(pl.multiple_of(place()[1] * half, 128), half)].T


def prepare(schur, inverse, first_cot):
    depth, width = schur.shape
    split = pltpu.VMEM((width, depth), BF16)
    return pl.pallas_call(
        prepare_kernel,
        out_shape=[
            split,
            split,
            pltpu.VMEM(inverse.shape, BF16),
            pltpu.VMEM((first_cot.shape[1] // 2, depth), F32),
        ],
        in_specs=[VMEM, VMEM, VMEM],
        out_specs=[VMEM] * 4,
        compiler_params=pltpu.CompilerParams(vmem_limit_bytes=12 * MIB),
        cost_estimate=pl.CostEstimate(flops=1024, bytes_accessed=1024, transcendentals=0),
        name="prepare",
    )(schur, inverse, first_cot)


def product_kernel(masks, cot, total, last, high, low, high2, low2, *rest):
    outs, value = rest[:-1], rest[-1]
    row, core, _ = place()
    width = high.shape[0]
    part = outs[0].shape[0]
    right = cot[...] - (total[...] + last[...].astype(F32))
    top = right.astype(BF16)
    rest_ = (right - top.astype(F32)).astype(BF16)
    for at, (a, b) in ((core, (high, low)), (1 - core, (high2, low2))):
        part_sum = dot_nt(a[...], top) + dot_nt(a[...], rest_) + dot_nt(b[...], top)
        value[pl.ds(pl.multiple_of(at * width, 16), width), :] = part_sum
    for mask, out in zip(masks, outs):
        piece = value[pl.ds(pl.multiple_of((row ^ mask) * part, 16), part), :]
        out[...] = piece.astype(out.dtype)


def product(masks, cot, total, last, high, low, high2, low2):
    half, depth = cot.shape
    width = high.shape[0]
    part = 2 * width // len(masks)
    outs = [pltpu.VMEM((part, half), BF16 if mask else F32) for mask in masks]
    return pl.pallas_call(
        functools.partial(product_kernel, masks),
        out_shape=outs,
        in_specs=[VMEM] * 7,
        out_specs=[VMEM] * len(outs),
        scratch_shapes=[pltpu.VMEM((2 * width, half), F32)],
        compiler_params=pltpu.CompilerParams(vmem_limit_bytes=12 * MIB),
        cost_estimate=pl.CostEstimate(flops=12 * width * depth * half, bytes_accessed=4 << 20, transcendentals=0),
        name="product",
    )(cot, total, last, high, low, high2, low2)


def recover_kernel(rows, first_primal, primal, cot, turned, *rest):
    blocks, near, rest = rest[:rows], rest[rows : rows + 2], rest[rows + 2 :]
    stacks, rest = rest[: 2 * rows], rest[2 * rows :]
    scen_adjoint, first_adjoint, grad, right, left, primals, update, adjoints, firsts, tile, arrived, gone = rest
    row, core, level = place()
    count, size, depth = blocks[0].shape
    total, directions = first_primal.shape
    half = directions // 2
    width = first_adjoint.shape[0]
    part = 2 * width // rows
    levels = stacks[0].shape[0] // part + 1
    loads = [
        pltpu.make_async_copy(first_primal, right.at[:, pl.ds(0, directions)], arrived.at[0]),
        pltpu.make_async_copy(primal, primals, arrived.at[1]),
    ]
    for load in loads:
        load.start()
    for side in range(2):
        lanes = pl.ds(pl.multiple_of(directions + (core ^ side) * half, 128), half)
        for mask in range(rows):
            for step in range(levels):
                start = (level ^ step) * (2 * width) + (row ^ mask) * part
                if step:
                    piece = stacks[side * rows + mask][(step - 1) * part : step * part, :]
                else:
                    piece = near[side][mask * part : (mask + 1) * part, :]
                right[pl.ds(pl.multiple_of(start, 16), part), lanes] = piece
    stores = []

    def store(source, target):
        stores.append(pltpu.make_async_copy(source, target, gone.at[len(stores)]))
        stores[-1].start()

    start = pl.multiple_of((level * 2 + core) * width, 16)
    firsts[...] = right[pl.ds(start, width), directions:].astype(F32)
    store(firsts, first_adjoint)
    for s in range(count):
        value = cot[s].astype(F32)
        for mask in range(rows):
            start = pl.multiple_of((row ^ mask) * depth, 128)
            value = value - dot(blocks[mask][s], right[pl.ds(start, depth), directions:])
        update[...] = value.astype(BF16)
        value = dot(turned[s], update[...])
        adjoints[s] = value
        store(adjoints.at[s], scen_adjoint.at[s])
        left[:, :directions] = -value.astype(BF16)
        if s == 0:
            for load in loads:
                load.wait()
        left[:, directions:] = -primals[s]
        for i in range(rows):
            slot = s * rows + i
            tile[slot] = dot_nt(left[...], right[i * depth : (i + 1) * depth, :])
            store(tile.at[slot], grad.at[s, :, pl.ds(i * depth, depth)])
    for copy in stores:
        copy.wait()


def recover(rows, first_primal, primal, cot, turned, blocks, stacks, width):
    count, size, depth = blocks[0].shape
    total, directions = first_primal.shape
    outs = [
        jax.ShapeDtypeStruct(cot.shape, F32),
        jax.ShapeDtypeStruct((width, directions), F32),
        jax.ShapeDtypeStruct((count, size, total), F32),
    ]
    inputs = [pltpu.with_memory_space_constraint(value, pltpu.HBM) for value in (first_primal, primal)]
    return pl.pallas_call(
        functools.partial(recover_kernel, rows),
        out_shape=outs,
        in_specs=[ANY, ANY] + [VMEM] * (2 + len(blocks) + len(stacks)),
        out_specs=[ANY, ANY, ANY],
        scratch_shapes=[
            pltpu.VMEM((total, 2 * directions), BF16),
            pltpu.VMEM((size, 2 * directions), BF16),
            pltpu.VMEM(primal.shape, BF16),
            pltpu.VMEM((size, directions), BF16),
            pltpu.VMEM(cot.shape, F32),
            pltpu.VMEM((width, directions), F32),
            pltpu.VMEM((count * rows, size, depth), F32),
            pltpu.SemaphoreType.DMA((2,)),
            pltpu.SemaphoreType.DMA((1 + count * (1 + rows),)),
        ],
        compiler_params=pltpu.CompilerParams(vmem_limit_bytes=28 * MIB),
        cost_estimate=pl.CostEstimate(
            flops=2 * count * size * directions * (3 * total + size), bytes_accessed=20 << 20, transcendentals=0
        ),
        name="recover",
    )(*inputs, cot, turned, *blocks, *stacks)


def body(scen_inverse, coupling, scen_cot, first_cot, schur_inverse, scen_primal, first_primal):
    rows, cols = lax.axis_size("row"), lax.axis_size("col")
    levels = cols // 2
    depth, width = schur_inverse.shape
    far = sorted(range(1, rows), key=lambda m: -bin(m).count("1"))

    blocks, arrived, helper = [None] * rows, [], None
    for group in (far, [0]):
        if not group:
            continue
        outs = condense(group, scen_inverse, scen_cot, coupling, helper, depth)
        if helper is None:
            helper, own_inverse, own_cot = outs[-3:]
        totals = []
        for i, mask in enumerate(group):
            keep, give, blocks[mask] = outs[3 * i : 3 * i + 3]
            totals.append(keep + swap(give, "col", 1).astype(F32))
        if group != [0]:
            ready = [total.astype(BF16) for total in totals]
            helper, *ready = lax.optimization_barrier((helper, *ready))
            arrived += [swap(value, "row", mask) for mask, value in zip(group, ready)]
    total = totals[0]
    for value in arrived:
        total = total + value.astype(F32)

    high, low, turned, cot_half = prepare(schur_inverse, own_inverse, first_cot)
    total, high, low, turned, cot_half = lax.optimization_barrier((total, high, low, turned, cot_half))
    high2, low2 = swap(high, "col", 1), swap(low, "col", 1)

    steps = [1 << i for i in range(1, cols.bit_length() - 1)]
    last = None
    for one, two in zip(steps, steps[::-1]):
        if last is not None:
            total = total + last.astype(F32)
        pairs = [(i, i ^ (two if i % 2 else one)) for i in range(cols)]
        last = lax.ppermute(total.astype(BF16), "col", pairs)

    pieces = product([0] + far, cot_half, total, last, high, low, high2, low2)
    mine = pieces[0]
    for mask, piece in zip(far, pieces[1:]):
        mine = mine + swap(piece, "row", mask).astype(F32)
    mine = mine.astype(BF16)

    stack = jnp.concatenate([swap(mine, "col", 2 * m) for m in range(1, levels)], 0)
    near, stacks = [mine] + [None] * (rows - 1), [stack] + [None] * (rows - 1)
    for mask in far:
        near[mask] = swap(mine, "row", mask)
        stacks[mask] = swap(stack, "row", mask)
    near = jnp.concatenate(near, 0)
    stacks = [near, swap(near, "col", 1)] + stacks + [swap(value, "col", 1) for value in stacks]
    scen_adjoint, first_adjoint, coupling_grad = recover(
        rows, first_primal, scen_primal, own_cot, turned, blocks, stacks, width
    )
    return (scen_adjoint, first_adjoint, coupling_grad)


def solution(mesh):
    return jax.shard_map(
        body,
        mesh=mesh,
        in_specs=(
            P(("row", "col"), None, None),
            P(("row", "col"), None, None),
            P(("row", "col"), None, None),
            P("row", None),
            P("row", "col"),
            P(("row", "col"), None, None),
            P(),
        ),
        out_specs=(P(("row", "col"), None, None), P("col", None), P(("row", "col"), None, None)),
        check_vma=False,
    )
```

```python
import functools

import jax
import jax.numpy as jnp
from jax import lax
from jax.experimental import pallas as pl
from jax.experimental.pallas import tpu as pltpu
from jax.sharding import PartitionSpec as P

F32 = jnp.float32
BF16 = jnp.bfloat16
VMEM = pl.BlockSpec(memory_space=pltpu.VMEM)
ANY = pl.BlockSpec(memory_space=pl.ANY)
MIB = 1024 * 1024


def swap(value, axis, mask):
    size = lax.axis_size(axis)
    return lax.ppermute(value, axis, [(i, i ^ mask) for i in range(size)])


def cross(value, masks):
    rows, cols = lax.axis_size("row"), lax.axis_size("col")
    pairs = [(r * cols + c, (r ^ masks[c % 2]) * cols + c) for r in range(rows) for c in range(cols)]
    return lax.ppermute(value, ("row", "col"), pairs)


def turned_by(core, mask):
    return mask ^ (3 * core) if lax.axis_size("row") == 4 and mask in (1, 2) else mask


def place():
    col = lax.axis_index("col")
    return lax.axis_index("row"), lax.rem(col, 2), lax.div(col, 2)


def dot(a, b):
    return jnp.dot(a, b, preferred_element_type=F32)


def dot_nt(a, b):
    return lax.dot_general(a, b, (((1,), (1,)), ((), ())), preferred_element_type=F32)


def dot_tn(a, b):
    return lax.dot_general(a, b, (((0,), (0,)), ((), ())), preferred_element_type=F32)


def condense_kernel(masks, first, *refs):
    row, core, _ = place()
    if first:
        inverse, cot, coupling, *refs = refs
        *outs, helper, own_inverse, own_cot, arrived = refs
    else:
        helper, coupling, *refs = refs
        *outs, arrived = refs
    keeps, gives, blocks = outs[0::3], outs[1::3], outs[2::3]
    count, size, depth = blocks[0].shape
    half = keeps[0].shape[0]
    copies = []
    if first:
        copies.append(pltpu.make_async_copy(cot, own_cot, arrived.at[0]))
        copies.append(pltpu.make_async_copy(inverse, own_inverse, arrived.at[1]))
    for i, mask in enumerate(masks):
        columns = pl.ds(pl.multiple_of((row ^ turned_by(core, mask)) * depth, 128), depth)
        copies.append(pltpu.make_async_copy(coupling.at[:, :, columns], blocks[i], arrived.at[2 + i]))
    for copy in copies:
        copy.start()
    if first:
        copies.pop(0).wait()
        copies.pop(0).wait()
        for s in range(count):
            value = dot_tn(own_cot[s], own_inverse[s]).astype(BF16)
            helper[core, :, s * size : (s + 1) * size] = value[:half]
            helper[1 - core, :, s * size : (s + 1) * size] = value[half:]
    left = helper[...].reshape(2 * half, count * size)
    for copy, keep, give, block in zip(copies, keeps, gives, blocks):
        copy.wait()
        value = dot(left, block[...].reshape(count * size, depth))
        keep[...] = value[:half]
        give[...] = value[half:].astype(BF16)


def condense(masks, inverse, cot, coupling, helper, depth):
    count, size, directions = cot.shape
    half = directions // 2
    first = helper is None
    outs = [pltpu.VMEM((half, depth), F32), pltpu.VMEM((half, depth), BF16), pltpu.VMEM((count, size, depth), BF16)]
    outs = outs * len(masks)
    inputs = [inverse, cot, coupling] if first else [coupling]
    inputs = [pltpu.with_memory_space_constraint(value, pltpu.HBM) for value in inputs]
    specs = [ANY] * len(inputs)
    if first:
        outs += [pltpu.VMEM((2, half, count * size), BF16)]
        outs += [pltpu.VMEM(inverse.shape, BF16), pltpu.VMEM(cot.shape, BF16)]
    else:
        inputs, specs = [helper] + inputs, [VMEM] + specs
    return pl.pallas_call(
        functools.partial(condense_kernel, masks, first),
        out_shape=outs,
        in_specs=specs,
        out_specs=[VMEM] * len(outs),
        scratch_shapes=[pltpu.SemaphoreType.DMA((2 + len(masks),))],
        compiler_params=pltpu.CompilerParams(vmem_limit_bytes=16 * MIB),
        cost_estimate=pl.CostEstimate(
            flops=2 * count * size * directions * depth * len(masks) if masks != [0] else 1024,
            bytes_accessed=(2 * len(masks)) << 20 if masks != [0] else 1024,
            transcendentals=0,
        ),
        name="condense",
    )(*inputs)


def prepare_kernel(schur, inverse, first_cot, high, low, turned, cot_half):
    half = cot_half.shape[0]
    value = schur[...].T
    top = value.astype(BF16)
    high[...] = top
    low[...] = (value - top.astype(F32)).astype(BF16)
    for s in range(inverse.shape[0]):
        turned[s] = inverse[s].astype(F32).T.astype(BF16)
    cot_half[...] = first_cot[:, pl.ds(pl.multiple_of(place()[1] * half, 128), half)].T


def prepare(schur, inverse, first_cot):
    depth, width = schur.shape
    split = pltpu.VMEM((width, depth), BF16)
    return pl.pallas_call(
        prepare_kernel,
        out_shape=[
            split,
            split,
            pltpu.VMEM(inverse.shape, BF16),
            pltpu.VMEM((first_cot.shape[1] // 2, depth), F32),
        ],
        in_specs=[VMEM, VMEM, VMEM],
        out_specs=[VMEM] * 4,
        compiler_params=pltpu.CompilerParams(vmem_limit_bytes=12 * MIB),
        cost_estimate=pl.CostEstimate(flops=1024, bytes_accessed=1024, transcendentals=0),
        name="prepare",
    )(schur, inverse, first_cot)


def product_kernel(masks, cot, total, last, high, low, high2, low2, *rest):
    outs, value = rest[:-1], rest[-1]
    row, core, _ = place()
    width = high.shape[0]
    part = outs[0].shape[0]
    right = cot[...] - (total[...] + last[...].astype(F32))
    top = right.astype(BF16)
    rest_ = (right - top.astype(F32)).astype(BF16)
    for at, (a, b) in ((core, (high, low)), (1 - core, (high2, low2))):
        part_sum = dot_nt(a[...], top) + dot_nt(a[...], rest_) + dot_nt(b[...], top)
        value[pl.ds(pl.multiple_of(at * width, 16), width), :] = part_sum
    for mask, out in zip(masks, outs):
        piece = value[pl.ds(pl.multiple_of((row ^ mask) * part, 16), part), :]
        out[...] = piece.astype(out.dtype)


def product(masks, cot, total, last, high, low, high2, low2):
    half, depth = cot.shape
    width = high.shape[0]
    part = 2 * width // len(masks)
    outs = [pltpu.VMEM((part, half), BF16 if mask else F32) for mask in masks]
    return pl.pallas_call(
        functools.partial(product_kernel, masks),
        out_shape=outs,
        in_specs=[VMEM] * 7,
        out_specs=[VMEM] * len(outs),
        scratch_shapes=[pltpu.VMEM((2 * width, half), F32)],
        compiler_params=pltpu.CompilerParams(vmem_limit_bytes=12 * MIB),
        cost_estimate=pl.CostEstimate(flops=12 * width * depth * half, bytes_accessed=4 << 20, transcendentals=0),
        name="product",
    )(cot, total, last, high, low, high2, low2)


def recover_kernel(rows, first_primal, primal, cot, turned, *rest):
    blocks, near, rest = rest[:rows], rest[rows : rows + 2], rest[rows + 2 :]
    stacks, rest = rest[: 2 * rows], rest[2 * rows :]
    scen_adjoint, first_adjoint, grad, right, left, primals, update, adjoints, firsts, tile, arrived, gone = rest
    row, core, level = place()
    count, size, depth = blocks[0].shape
    total, directions = first_primal.shape
    half = directions // 2
    width = first_adjoint.shape[0]
    part = 2 * width // rows
    levels = stacks[0].shape[0] // part + 1
    loads = [
        pltpu.make_async_copy(first_primal, right.at[:, pl.ds(0, directions)], arrived.at[0]),
        pltpu.make_async_copy(primal, primals, arrived.at[1]),
    ]
    for load in loads:
        load.start()
    for side in range(2):
        lanes = pl.ds(pl.multiple_of(directions + (core ^ side) * half, 128), half)
        for mask in range(rows):
            for step in range(levels):
                start = (level ^ step) * (2 * width) + (row ^ mask) * part
                if step:
                    piece = stacks[side * rows + mask][(step - 1) * part : step * part, :]
                else:
                    piece = near[side][mask * part : (mask + 1) * part, :]
                right[pl.ds(pl.multiple_of(start, 16), part), lanes] = piece
    stores = []

    def store(source, target):
        stores.append(pltpu.make_async_copy(source, target, gone.at[len(stores)]))
        stores[-1].start()

    start = pl.multiple_of((level * 2 + core) * width, 16)
    firsts[...] = right[pl.ds(start, width), directions:].astype(F32)
    store(firsts, first_adjoint)
    for s in range(count):
        value = cot[s].astype(F32)
        for mask in range(rows):
            start = pl.multiple_of((row ^ turned_by(core, mask)) * depth, 128)
            value = value - dot(blocks[mask][s], right[pl.ds(start, depth), directions:])
        update[...] = value.astype(BF16)
        value = dot(turned[s], update[...])
        adjoints[s] = value
        store(adjoints.at[s], scen_adjoint.at[s])
        left[:, :directions] = -value.astype(BF16)
        if s == 0:
            for load in loads:
                load.wait()
        left[:, directions:] = -primals[s]
        for i in range(rows):
            slot = s * rows + i
            tile[slot] = dot_nt(left[...], right[i * depth : (i + 1) * depth, :])
            store(tile.at[slot], grad.at[s, :, pl.ds(i * depth, depth)])
    for copy in stores:
        copy.wait()


def recover(rows, first_primal, primal, cot, turned, blocks, stacks, width):
    count, size, depth = blocks[0].shape
    total, directions = first_primal.shape
    outs = [
        jax.ShapeDtypeStruct(cot.shape, F32),
        jax.ShapeDtypeStruct((width, directions), F32),
        jax.ShapeDtypeStruct((count, size, total), F32),
    ]
    inputs = [pltpu.with_memory_space_constraint(value, pltpu.HBM) for value in (first_primal, primal)]
    return pl.pallas_call(
        functools.partial(recover_kernel, rows),
        out_shape=outs,
        in_specs=[ANY, ANY] + [VMEM] * (2 + len(blocks) + len(stacks)),
        out_specs=[ANY, ANY, ANY],
        scratch_shapes=[
            pltpu.VMEM((total, 2 * directions), BF16),
            pltpu.VMEM((size, 2 * directions), BF16),
            pltpu.VMEM(primal.shape, BF16),
            pltpu.VMEM((size, directions), BF16),
            pltpu.VMEM(cot.shape, F32),
            pltpu.VMEM((width, directions), F32),
            pltpu.VMEM((count * rows, size, depth), F32),
            pltpu.SemaphoreType.DMA((2,)),
            pltpu.SemaphoreType.DMA((1 + count * (1 + rows),)),
        ],
        compiler_params=pltpu.CompilerParams(vmem_limit_bytes=28 * MIB),
        cost_estimate=pl.CostEstimate(
            flops=2 * count * size * directions * (3 * total + size), bytes_accessed=20 << 20, transcendentals=0
        ),
        name="recover",
    )(*inputs, cot, turned, *blocks, *stacks)


def body(scen_inverse, coupling, scen_cot, first_cot, schur_inverse, scen_primal, first_primal):
    rows, cols = lax.axis_size("row"), lax.axis_size("col")
    levels = cols // 2
    depth, width = schur_inverse.shape
    far = sorted(range(1, rows), key=lambda m: -bin(m).count("1"))

    blocks = [None] * rows
    outs = condense(far, scen_inverse, scen_cot, coupling, None, depth)
    helper, own_inverse, own_cot = outs[-3:]
    keeps, gives = [None] * rows, [None] * rows
    for i, mask in enumerate(far):
        keeps[mask], gives[mask], blocks[mask] = outs[3 * i : 3 * i + 3]

    def chip(mask):
        return keeps[mask] + swap(gives[int(turned_by(1, mask))], "col", 1).astype(F32)

    terms = {mask: chip(mask) for mask in far}
    ready = {mask: terms[mask].astype(BF16) for mask in far}
    helper, *values = lax.optimization_barrier((helper, *ready.values()))
    ready = dict(zip(far, values))
    keeps[0], gives[0], blocks[0] = condense([0], scen_inverse, scen_cot, coupling, helper, depth)
    total = chip(0)
    if rows == 4:
        through = cross(ready[3], (1, 2))
        near = cross(ready[1], (1, 2))
        passed = (terms[2] + through.astype(F32)).astype(BF16)
        own_inverse, passed = lax.optimization_barrier((own_inverse, passed))
        arrived = [near, cross(passed, (2, 1))]
    else:
        arrived = [swap(ready[mask], "row", mask) for mask in far]
    for value in arrived:
        total = total + value.astype(F32)

    high, low, turned, cot_half = prepare(schur_inverse, own_inverse, first_cot)
    total, high, low, turned, cot_half = lax.optimization_barrier((total, high, low, turned, cot_half))
    high2, low2 = swap(high, "col", 1), swap(low, "col", 1)

    mask = 2
    last = None
    while mask < cols:
        if last is not None:
            total = total + last.astype(F32)
        last = swap(total.astype(BF16), "col", mask if 2 * mask < cols else cols - 2)
        mask *= 2

    pieces = product([0] + far, cot_half, total, last, high, low, high2, low2)
    mine = pieces[0]
    for mask, piece in zip(far, pieces[1:]):
        mine = mine + swap(piece, "row", mask).astype(F32)
    mine = mine.astype(BF16)

    stack = jnp.concatenate([swap(mine, "col", 2 * m) for m in range(1, levels)], 0)
    near, stacks = [mine] + [None] * (rows - 1), [stack] + [None] * (rows - 1)
    for mask in far:
        near[mask] = swap(mine, "row", mask)
        stacks[mask] = swap(stack, "row", mask)
    near = jnp.concatenate(near, 0)
    stacks = [near, swap(near, "col", 1)] + stacks + [swap(value, "col", 1) for value in stacks]
    scen_adjoint, first_adjoint, coupling_grad = recover(
        rows, first_primal, scen_primal, own_cot, turned, blocks, stacks, width
    )
    return (scen_adjoint, first_adjoint, coupling_grad)


def solution(mesh):
    return jax.shard_map(
        body,
        mesh=mesh,
        in_specs=(
            P(("row", "col"), None, None),
            P(("row", "col"), None, None),
            P(("row", "col"), None, None),
            P("row", None),
            P("row", "col"),
            P(("row", "col"), None, None),
            P(),
        ),
        out_specs=(P(("row", "col"), None, None), P("col", None), P(("row", "col"), None, None)),
        check_vma=False,
    )
```

```python
import functools

import jax
import jax.numpy as jnp
from jax import lax
from jax.experimental import pallas as pl
from jax.experimental.pallas import tpu as pltpu
from jax.sharding import PartitionSpec as P

F32 = jnp.float32
BF16 = jnp.bfloat16
VMEM = pl.BlockSpec(memory_space=pltpu.VMEM)
ANY = pl.BlockSpec(memory_space=pl.ANY)
MIB = 1024 * 1024


def swap(value, axis, mask):
    size = lax.axis_size(axis)
    return lax.ppermute(value, axis, [(i, i ^ mask) for i in range(size)])


def cross(value, masks):
    rows, cols = lax.axis_size("row"), lax.axis_size("col")
    pairs = [(r * cols + c, (r ^ masks[c % 2]) * cols + c) for r in range(rows) for c in range(cols)]
    return lax.ppermute(value, ("row", "col"), pairs)


def turned_by(core, mask):
    return mask ^ (3 * core) if lax.axis_size("row") == 4 and mask in (1, 2) else mask


def place():
    col = lax.axis_index("col")
    return lax.axis_index("row"), lax.rem(col, 2), lax.div(col, 2)


def dot(a, b):
    return jnp.dot(a, b, preferred_element_type=F32)


def dot_nt(a, b):
    return lax.dot_general(a, b, (((1,), (1,)), ((), ())), preferred_element_type=F32)


def dot_tn(a, b):
    return lax.dot_general(a, b, (((0,), (0,)), ((), ())), preferred_element_type=F32)


def condense_kernel(masks, first, *refs):
    row, core, _ = place()
    if first:
        inverse, cot, coupling, *refs = refs
        *outs, helper, own_inverse, own_cot, arrived = refs
    else:
        helper, coupling, *refs = refs
        *outs, arrived = refs
    keeps, gives, blocks = outs[0::3], outs[1::3], outs[2::3]
    count, size, depth = blocks[0].shape
    half = keeps[0].shape[0]
    copies = []
    if first:
        copies.append(pltpu.make_async_copy(cot, own_cot, arrived.at[0]))
        copies.append(pltpu.make_async_copy(inverse, own_inverse, arrived.at[1]))
    for i, mask in enumerate(masks):
        columns = pl.ds(pl.multiple_of((row ^ turned_by(core, mask)) * depth, 128), depth)
        copies.append(pltpu.make_async_copy(coupling.at[:, :, columns], blocks[i], arrived.at[2 + i]))
    for copy in copies:
        copy.start()
    if first:
        copies.pop(0).wait()
        copies.pop(0).wait()
        for s in range(count):
            value = dot_tn(own_cot[s], own_inverse[s]).astype(BF16)
            helper[core, :, s * size : (s + 1) * size] = value[:half]
            helper[1 - core, :, s * size : (s + 1) * size] = value[half:]
    left = helper[...].reshape(2 * half, count * size)
    for copy, keep, give, block in zip(copies, keeps, gives, blocks):
        copy.wait()
        value = dot(left, block[...].reshape(count * size, depth))
        keep[...] = value[:half]
        give[...] = value[half:].astype(BF16)


def condense(masks, inverse, cot, coupling, helper, depth):
    count, size, directions = cot.shape
    half = directions // 2
    first = helper is None
    outs = [pltpu.VMEM((half, depth), F32), pltpu.VMEM((half, depth), BF16), pltpu.VMEM((count, size, depth), BF16)]
    outs = outs * len(masks)
    inputs = [inverse, cot, coupling] if first else [coupling]
    inputs = [pltpu.with_memory_space_constraint(value, pltpu.HBM) for value in inputs]
    specs = [ANY] * len(inputs)
    if first:
        outs += [pltpu.VMEM((2, half, count * size), BF16)]
        outs += [pltpu.VMEM(inverse.shape, BF16), pltpu.VMEM(cot.shape, BF16)]
    else:
        inputs, specs = [helper] + inputs, [VMEM] + specs
    return pl.pallas_call(
        functools.partial(condense_kernel, masks, first),
        out_shape=outs,
        in_specs=specs,
        out_specs=[VMEM] * len(outs),
        scratch_shapes=[pltpu.SemaphoreType.DMA((2 + len(masks),))],
        compiler_params=pltpu.CompilerParams(vmem_limit_bytes=16 * MIB),
        cost_estimate=pl.CostEstimate(
            flops=2 * count * size * directions * depth * len(masks) if masks != [0] else 1024,
            bytes_accessed=(2 * len(masks)) << 20 if masks != [0] else 1024,
            transcendentals=0,
        ),
        name="condense",
    )(*inputs)


def prepare_kernel(schur, inverse, first_cot, high, low, turned, cot_half):
    half = cot_half.shape[0]
    value = schur[...].T
    top = value.astype(BF16)
    high[...] = top
    low[...] = (value - top.astype(F32)).astype(BF16)
    for s in range(inverse.shape[0]):
        turned[s] = inverse[s].astype(F32).T.astype(BF16)
    cot_half[...] = first_cot[:, pl.ds(pl.multiple_of(place()[1] * half, 128), half)].T


def prepare(schur, inverse, first_cot):
    depth, width = schur.shape
    split = pltpu.VMEM((width, depth), BF16)
    return pl.pallas_call(
        prepare_kernel,
        out_shape=[
            split,
            split,
            pltpu.VMEM(inverse.shape, BF16),
            pltpu.VMEM((first_cot.shape[1] // 2, depth), F32),
        ],
        in_specs=[VMEM, VMEM, VMEM],
        out_specs=[VMEM] * 4,
        compiler_params=pltpu.CompilerParams(vmem_limit_bytes=12 * MIB),
        cost_estimate=pl.CostEstimate(flops=1024, bytes_accessed=1024, transcendentals=0),
        name="prepare",
    )(schur, inverse, first_cot)


def product_kernel(masks, cot, total, last, high, low, high2, low2, *rest):
    outs, value = rest[:-1], rest[-1]
    row, core, _ = place()
    width = high.shape[0]
    part = outs[0].shape[0]
    right = cot[...] - (total[...] + last[...].astype(F32))
    top = right.astype(BF16)
    rest_ = (right - top.astype(F32)).astype(BF16)
    for at, (a, b) in ((core, (high, low)), (1 - core, (high2, low2))):
        part_sum = dot_nt(a[...], top) + dot_nt(a[...], rest_) + dot_nt(b[...], top)
        value[pl.ds(pl.multiple_of(at * width, 16), width), :] = part_sum
    for mask, out in zip(masks, outs):
        piece = value[pl.ds(pl.multiple_of((row ^ mask) * part, 16), part), :]
        out[...] = piece.astype(out.dtype)


def product(masks, cot, total, last, high, low, high2, low2):
    half, depth = cot.shape
    width = high.shape[0]
    part = 2 * width // len(masks)
    outs = [pltpu.VMEM((part, half), BF16 if mask else F32) for mask in masks]
    return pl.pallas_call(
        functools.partial(product_kernel, masks),
        out_shape=outs,
        in_specs=[VMEM] * 7,
        out_specs=[VMEM] * len(outs),
        scratch_shapes=[pltpu.VMEM((2 * width, half), F32)],
        compiler_params=pltpu.CompilerParams(vmem_limit_bytes=12 * MIB),
        cost_estimate=pl.CostEstimate(flops=12 * width * depth * half, bytes_accessed=4 << 20, transcendentals=0),
        name="product",
    )(cot, total, last, high, low, high2, low2)


def recover_kernel(rows, first_primal, primal, cot, turned, *rest):
    blocks, rest = rest[:rows], rest[rows:]
    stacks, rest = rest[: 2 * rows], rest[2 * rows :]
    scen_adjoint, first_adjoint, grad, right, left, primals, update, adjoints, firsts, tile, arrived, gone = rest
    row, core, level = place()
    count, size, depth = blocks[0].shape
    total, directions = first_primal.shape
    half = directions // 2
    width = first_adjoint.shape[0]
    part = 2 * width // rows
    levels = stacks[0].shape[0] // part
    loads = [
        pltpu.make_async_copy(first_primal, right.at[:, pl.ds(0, directions)], arrived.at[0]),
        pltpu.make_async_copy(primal, primals, arrived.at[1]),
    ]
    for load in loads:
        load.start()
    for side in range(2):
        lanes = pl.ds(pl.multiple_of(directions + (core ^ side) * half, 128), half)
        for mask in range(rows):
            for step in range(levels):
                start = (level ^ step) * (2 * width) + (row ^ mask) * part
                piece = stacks[side * rows + mask][step * part : (step + 1) * part, :]
                right[pl.ds(pl.multiple_of(start, 16), part), lanes] = piece
    stores = []

    def store(source, target):
        stores.append(pltpu.make_async_copy(source, target, gone.at[len(stores)]))
        stores[-1].start()

    start = pl.multiple_of((level * 2 + core) * width, 16)
    firsts[...] = right[pl.ds(start, width), directions:].astype(F32)
    store(firsts, first_adjoint)
    for s in range(count):
        value = cot[s].astype(F32)
        for mask in range(rows):
            start = pl.multiple_of((row ^ turned_by(core, mask)) * depth, 128)
            value = value - dot(blocks[mask][s], right[pl.ds(start, depth), directions:])
        update[...] = value.astype(BF16)
        value = dot(turned[s], update[...])
        adjoints[s] = value
        store(adjoints.at[s], scen_adjoint.at[s])
        left[:, :directions] = -value.astype(BF16)
        if s == 0:
            for load in loads:
                load.wait()
        left[:, directions:] = -primals[s]
        for i in range(rows):
            slot = s * rows + i
            tile[slot] = dot_nt(left[...], right[i * depth : (i + 1) * depth, :])
            store(tile.at[slot], grad.at[s, :, pl.ds(i * depth, depth)])
    for copy in stores:
        copy.wait()


def recover(rows, first_primal, primal, cot, turned, blocks, stacks, width):
    count, size, depth = blocks[0].shape
    total, directions = first_primal.shape
    outs = [
        jax.ShapeDtypeStruct(cot.shape, F32),
        jax.ShapeDtypeStruct((width, directions), F32),
        jax.ShapeDtypeStruct((count, size, total), F32),
    ]
    inputs = [pltpu.with_memory_space_constraint(value, pltpu.HBM) for value in (first_primal, primal)]
    return pl.pallas_call(
        functools.partial(recover_kernel, rows),
        out_shape=outs,
        in_specs=[ANY, ANY] + [VMEM] * (2 + len(blocks) + len(stacks)),
        out_specs=[ANY, ANY, ANY],
        scratch_shapes=[
            pltpu.VMEM((total, 2 * directions), BF16),
            pltpu.VMEM((size, 2 * directions), BF16),
            pltpu.VMEM(primal.shape, BF16),
            pltpu.VMEM((size, directions), BF16),
            pltpu.VMEM(cot.shape, F32),
            pltpu.VMEM((width, directions), F32),
            pltpu.VMEM((count * rows, size, depth), F32),
            pltpu.SemaphoreType.DMA((2,)),
            pltpu.SemaphoreType.DMA((1 + count * (1 + rows),)),
        ],
        compiler_params=pltpu.CompilerParams(vmem_limit_bytes=28 * MIB),
        cost_estimate=pl.CostEstimate(
            flops=2 * count * size * directions * (3 * total + size), bytes_accessed=20 << 20, transcendentals=0
        ),
        name="recover",
    )(*inputs, cot, turned, *blocks, *stacks)


def body(scen_inverse, coupling, scen_cot, first_cot, schur_inverse, scen_primal, first_primal):
    rows, cols = lax.axis_size("row"), lax.axis_size("col")
    levels = cols // 2
    depth, width = schur_inverse.shape
    far = sorted(range(1, rows), key=lambda m: -bin(m).count("1"))

    blocks = [None] * rows
    outs = condense(far, scen_inverse, scen_cot, coupling, None, depth)
    helper, own_inverse, own_cot = outs[-3:]
    keeps, gives = [None] * rows, [None] * rows
    for i, mask in enumerate(far):
        keeps[mask], gives[mask], blocks[mask] = outs[3 * i : 3 * i + 3]

    def chip(mask):
        return keeps[mask] + swap(gives[int(turned_by(1, mask))], "col", 1).astype(F32)

    terms = {mask: chip(mask) for mask in far}
    ready = {mask: terms[mask].astype(BF16) for mask in far}
    helper, *values = lax.optimization_barrier((helper, *ready.values()))
    ready = dict(zip(far, values))
    keeps[0], gives[0], blocks[0] = condense([0], scen_inverse, scen_cot, coupling, helper, depth)
    total = chip(0)
    if rows == 4:
        through = cross(ready[3], (1, 2))
        near = cross(ready[1], (1, 2))
        passed = (terms[2] + through.astype(F32)).astype(BF16)
        own_inverse, passed = lax.optimization_barrier((own_inverse, passed))
        arrived = [near, cross(passed, (2, 1))]
    else:
        arrived = [swap(ready[mask], "row", mask) for mask in far]
    for value in arrived:
        total = total + value.astype(F32)

    high, low, turned, cot_half = prepare(schur_inverse, own_inverse, first_cot)
    total, high, low, turned, cot_half = lax.optimization_barrier((total, high, low, turned, cot_half))
    high2, low2 = swap(high, "col", 1), swap(low, "col", 1)

    mask = 2
    last = None
    while mask < cols:
        if last is not None:
            total = total + last.astype(F32)
        last = swap(total.astype(BF16), "col", mask if 2 * mask < cols else cols - 2)
        mask *= 2

    pieces = product([0] + far, cot_half, total, last, high, low, high2, low2)
    mine = pieces[0]
    for mask, piece in zip(far, pieces[1:]):
        mine = mine + swap(piece, "row", mask).astype(F32)
    mine = mine.astype(BF16)

    stack = jnp.concatenate([mine] + [swap(mine, "col", 2 * m) for m in range(1, levels)], 0)
    stacks = [stack] + [None] * (rows - 1)
    for mask in far:
        stacks[mask] = swap(stack, "row", mask)
    stacks = stacks + [swap(value, "col", 1) for value in stacks]
    scen_adjoint, first_adjoint, coupling_grad = recover(
        rows, first_primal, scen_primal, own_cot, turned, blocks, stacks, width
    )
    return (scen_adjoint, first_adjoint, coupling_grad)


def solution(mesh):
    return jax.shard_map(
        body,
        mesh=mesh,
        in_specs=(
            P(("row", "col"), None, None),
            P(("row", "col"), None, None),
            P(("row", "col"), None, None),
            P("row", None),
            P("row", "col"),
            P(("row", "col"), None, None),
            P(),
        ),
        out_specs=(P(("row", "col"), None, None), P("col", None), P(("row", "col"), None, None)),
        check_vma=False,
    )
```

```python
import functools

import jax
import jax.numpy as jnp
from jax import lax
from jax.experimental import pallas as pl
from jax.experimental.pallas import tpu as pltpu
from jax.sharding import PartitionSpec as P

F32 = jnp.float32
BF16 = jnp.bfloat16
VMEM = pl.BlockSpec(memory_space=pltpu.VMEM)
ANY = pl.BlockSpec(memory_space=pl.ANY)
MIB = 1024 * 1024


def swap(value, axis, mask):
    size = lax.axis_size(axis)
    return lax.ppermute(value, axis, [(i, i ^ mask) for i in range(size)])


def cross(value, masks):
    rows, cols = lax.axis_size("row"), lax.axis_size("col")
    pairs = [(r * cols + c, (r ^ masks[c % 2]) * cols + c) for r in range(rows) for c in range(cols)]
    return lax.ppermute(value, ("row", "col"), pairs)


def turned_by(core, mask):
    return mask ^ (3 * core) if lax.axis_size("row") == 4 and mask in (1, 2) else mask


def place():
    col = lax.axis_index("col")
    return lax.axis_index("row"), lax.rem(col, 2), lax.div(col, 2)


def dot(a, b):
    return jnp.dot(a, b, preferred_element_type=F32)


def dot_nt(a, b):
    return lax.dot_general(a, b, (((1,), (1,)), ((), ())), preferred_element_type=F32)


def dot_tn(a, b):
    return lax.dot_general(a, b, (((0,), (0,)), ((), ())), preferred_element_type=F32)


def condense_kernel(masks, first, *refs):
    row, core, _ = place()
    if first:
        inverse, cot, coupling, *refs = refs
        *outs, helper, own_inverse, own_cot, arrived = refs
    else:
        helper, coupling, *refs = refs
        *outs, arrived = refs
    keeps, gives, blocks = outs[0::3], outs[1::3], outs[2::3]
    count, size, depth = blocks[0].shape
    half = keeps[0].shape[0]
    copies = []
    if first:
        copies.append(pltpu.make_async_copy(cot, own_cot, arrived.at[0]))
        copies.append(pltpu.make_async_copy(inverse, own_inverse, arrived.at[1]))
    for i, mask in enumerate(masks):
        columns = pl.ds(pl.multiple_of((row ^ turned_by(core, mask)) * depth, 128), depth)
        copies.append(pltpu.make_async_copy(coupling.at[:, :, columns], blocks[i], arrived.at[2 + i]))
    for copy in copies:
        copy.start()
    if first:
        copies.pop(0).wait()
        copies.pop(0).wait()
        for s in range(count):
            value = dot_tn(own_cot[s], own_inverse[s]).astype(BF16)
            helper[core, :, s * size : (s + 1) * size] = value[:half]
            helper[1 - core, :, s * size : (s + 1) * size] = value[half:]
    left = helper[...].reshape(2 * half, count * size)
    for copy, keep, give, block in zip(copies, keeps, gives, blocks):
        copy.wait()
        value = dot(left, block[...].reshape(count * size, depth))
        keep[...] = value[:half]
        give[...] = value[half:].astype(BF16)


def condense(masks, inverse, cot, coupling, helper, depth):
    count, size, directions = cot.shape
    half = directions // 2
    first = helper is None
    outs = [pltpu.VMEM((half, depth), F32), pltpu.VMEM((half, depth), BF16), pltpu.VMEM((count, size, depth), BF16)]
    outs = outs * len(masks)
    inputs = [inverse, cot, coupling] if first else [coupling]
    inputs = [pltpu.with_memory_space_constraint(value, pltpu.HBM) for value in inputs]
    specs = [ANY] * len(inputs)
    if first:
        outs += [pltpu.VMEM((2, half, count * size), BF16)]
        outs += [pltpu.VMEM(inverse.shape, BF16), pltpu.VMEM(cot.shape, BF16)]
    else:
        inputs, specs = [helper] + inputs, [VMEM] + specs
    return pl.pallas_call(
        functools.partial(condense_kernel, masks, first),
        out_shape=outs,
        in_specs=specs,
        out_specs=[VMEM] * len(outs),
        scratch_shapes=[pltpu.SemaphoreType.DMA((2 + len(masks),))],
        compiler_params=pltpu.CompilerParams(vmem_limit_bytes=16 * MIB),
        cost_estimate=pl.CostEstimate(
            flops=2 * count * size * directions * depth * len(masks) if masks != [0] else 1024,
            bytes_accessed=(2 * len(masks)) << 20 if masks != [0] else 1024,
            transcendentals=0,
        ),
        name="condense",
    )(*inputs)


def prepare_kernel(schur, inverse, first_cot, high, low, turned, cot_half):
    half = cot_half.shape[0]
    value = schur[...].T
    top = value.astype(BF16)
    high[...] = top
    low[...] = (value - top.astype(F32)).astype(BF16)
    for s in range(inverse.shape[0]):
        turned[s] = inverse[s].astype(F32).T.astype(BF16)
    cot_half[...] = first_cot[:, pl.ds(pl.multiple_of(place()[1] * half, 128), half)].T


def prepare(schur, inverse, first_cot):
    depth, width = schur.shape
    split = pltpu.VMEM((width, depth), BF16)
    return pl.pallas_call(
        prepare_kernel,
        out_shape=[
            split,
            split,
            pltpu.VMEM(inverse.shape, BF16),
            pltpu.VMEM((first_cot.shape[1] // 2, depth), F32),
        ],
        in_specs=[VMEM, VMEM, VMEM],
        out_specs=[VMEM] * 4,
        compiler_params=pltpu.CompilerParams(vmem_limit_bytes=12 * MIB),
        cost_estimate=pl.CostEstimate(flops=1024, bytes_accessed=1024, transcendentals=0),
        name="prepare",
    )(schur, inverse, first_cot)


def product_kernel(masks, cot, total, last, high, low, high2, low2, *rest):
    outs, value = rest[:-1], rest[-1]
    row, core, _ = place()
    width = high.shape[0]
    part = outs[0].shape[0]
    right = cot[...] - (total[...] + last[...].astype(F32))
    top = right.astype(BF16)
    both = jnp.concatenate([top, (right - top.astype(F32)).astype(BF16)], 0)
    for at, (a, b) in ((core, (high, low)), (1 - core, (high2, low2))):
        wide = dot_nt(a[...], both)
        part_sum = wide[:, : wide.shape[1] // 2] + wide[:, wide.shape[1] // 2 :] + dot_nt(b[...], top)
        value[pl.ds(pl.multiple_of(at * width, 16), width), :] = part_sum
    for mask, out in zip(masks, outs):
        piece = value[pl.ds(pl.multiple_of((row ^ mask) * part, 16), part), :]
        out[...] = piece.astype(out.dtype)


def product(masks, cot, total, last, high, low, high2, low2):
    half, depth = cot.shape
    width = high.shape[0]
    part = 2 * width // len(masks)
    outs = [pltpu.VMEM((part, half), BF16 if mask else F32) for mask in masks]
    return pl.pallas_call(
        functools.partial(product_kernel, masks),
        out_shape=outs,
        in_specs=[VMEM] * 7,
        out_specs=[VMEM] * len(outs),
        scratch_shapes=[pltpu.VMEM((2 * width, half), F32)],
        compiler_params=pltpu.CompilerParams(vmem_limit_bytes=12 * MIB),
        cost_estimate=pl.CostEstimate(flops=12 * width * depth * half, bytes_accessed=4 << 20, transcendentals=0),
        name="product",
    )(cot, total, last, high, low, high2, low2)


def recover_kernel(rows, first_primal, primal, cot, turned, *rest):
    blocks, rest = rest[:rows], rest[rows:]
    stacks, rest = rest[: 2 * rows], rest[2 * rows :]
    scen_adjoint, first_adjoint, grad, right, left, primals, update, adjoints, firsts, tile, arrived, gone = rest
    row, core, level = place()
    count, size, depth = blocks[0].shape
    total, directions = first_primal.shape
    half = directions // 2
    width = first_adjoint.shape[0]
    part = 2 * width // rows
    levels = stacks[0].shape[0] // part
    loads = [
        pltpu.make_async_copy(first_primal, right.at[:, pl.ds(0, directions)], arrived.at[0]),
        pltpu.make_async_copy(primal, primals, arrived.at[1]),
    ]
    for load in loads:
        load.start()
    for side in range(2):
        lanes = pl.ds(pl.multiple_of(directions + (core ^ side) * half, 128), half)
        for mask in range(rows):
            for step in range(levels):
                start = (level ^ step) * (2 * width) + (row ^ mask) * part
                piece = stacks[side * rows + mask][step * part : (step + 1) * part, :]
                right[pl.ds(pl.multiple_of(start, 16), part), lanes] = piece
    stores = []

    def store(source, target):
        stores.append(pltpu.make_async_copy(source, target, gone.at[len(stores)]))
        stores[-1].start()

    start = pl.multiple_of((level * 2 + core) * width, 16)
    firsts[...] = right[pl.ds(start, width), directions:].astype(F32)
    store(firsts, first_adjoint)
    for s in range(count):
        value = cot[s].astype(F32)
        for mask in range(rows):
            start = pl.multiple_of((row ^ turned_by(core, mask)) * depth, 128)
            value = value - dot(blocks[mask][s], right[pl.ds(start, depth), directions:])
        update[...] = value.astype(BF16)
        value = dot(turned[s], update[...])
        adjoints[s] = value
        store(adjoints.at[s], scen_adjoint.at[s])
        left[:, :directions] = -value.astype(BF16)
        if s == 0:
            for load in loads:
                load.wait()
        left[:, directions:] = -primals[s]
        for i in range(rows):
            slot = s * rows + i
            tile[slot] = dot_nt(left[...], right[i * depth : (i + 1) * depth, :])
            store(tile.at[slot], grad.at[s, :, pl.ds(i * depth, depth)])
    for copy in stores:
        copy.wait()


def recover(rows, first_primal, primal, cot, turned, blocks, stacks, width):
    count, size, depth = blocks[0].shape
    total, directions = first_primal.shape
    outs = [
        jax.ShapeDtypeStruct(cot.shape, F32),
        jax.ShapeDtypeStruct((width, directions), F32),
        jax.ShapeDtypeStruct((count, size, total), F32),
    ]
    inputs = [pltpu.with_memory_space_constraint(value, pltpu.HBM) for value in (first_primal, primal)]
    return pl.pallas_call(
        functools.partial(recover_kernel, rows),
        out_shape=outs,
        in_specs=[ANY, ANY] + [VMEM] * (2 + len(blocks) + len(stacks)),
        out_specs=[ANY, ANY, ANY],
        scratch_shapes=[
            pltpu.VMEM((total, 2 * directions), BF16),
            pltpu.VMEM((size, 2 * directions), BF16),
            pltpu.VMEM(primal.shape, BF16),
            pltpu.VMEM((size, directions), BF16),
            pltpu.VMEM(cot.shape, F32),
            pltpu.VMEM((width, directions), F32),
            pltpu.VMEM((count * rows, size, depth), F32),
            pltpu.SemaphoreType.DMA((2,)),
            pltpu.SemaphoreType.DMA((1 + count * (1 + rows),)),
        ],
        compiler_params=pltpu.CompilerParams(vmem_limit_bytes=28 * MIB),
        cost_estimate=pl.CostEstimate(
            flops=2 * count * size * directions * (3 * total + size), bytes_accessed=20 << 20, transcendentals=0
        ),
        name="recover",
    )(*inputs, cot, turned, *blocks, *stacks)


def body(scen_inverse, coupling, scen_cot, first_cot, schur_inverse, scen_primal, first_primal):
    rows, cols = lax.axis_size("row"), lax.axis_size("col")
    levels = cols // 2
    depth, width = schur_inverse.shape
    far = sorted(range(1, rows), key=lambda m: -bin(m).count("1"))

    blocks = [None] * rows
    outs = condense(far, scen_inverse, scen_cot, coupling, None, depth)
    helper, own_inverse, own_cot = outs[-3:]
    keeps, gives = [None] * rows, [None] * rows
    for i, mask in enumerate(far):
        keeps[mask], gives[mask], blocks[mask] = outs[3 * i : 3 * i + 3]

    def chip(mask):
        return keeps[mask] + swap(gives[int(turned_by(1, mask))], "col", 1).astype(F32)

    terms = {mask: chip(mask) for mask in far}
    ready = {mask: terms[mask].astype(BF16) for mask in far}
    helper, *values = lax.optimization_barrier((helper, *ready.values()))
    ready = dict(zip(far, values))
    keeps[0], gives[0], blocks[0] = condense([0], scen_inverse, scen_cot, coupling, helper, depth)
    total = chip(0)
    if rows == 4:
        through = cross(ready[3], (1, 2))
        near = cross(ready[1], (1, 2))
        passed = (terms[2] + through.astype(F32)).astype(BF16)
        own_inverse, passed = lax.optimization_barrier((own_inverse, passed))
        arrived = [near, cross(passed, (2, 1))]
    else:
        arrived = [swap(ready[mask], "row", mask) for mask in far]
    for value in arrived:
        total = total + value.astype(F32)

    high, low, turned, cot_half = prepare(schur_inverse, own_inverse, first_cot)
    total, high, low, turned, cot_half = lax.optimization_barrier((total, high, low, turned, cot_half))
    high2, low2 = swap(high, "col", 1), swap(low, "col", 1)

    mask = 2
    last = None
    while mask < cols:
        if last is not None:
            total = total + last.astype(F32)
        last = swap(total.astype(BF16), "col", mask if 2 * mask < cols else cols - 2)
        mask *= 2

    pieces = product([0] + far, cot_half, total, last, high, low, high2, low2)
    mine = pieces[0]
    for mask, piece in zip(far, pieces[1:]):
        mine = mine + swap(piece, "row", mask).astype(F32)
    mine = mine.astype(BF16)

    stack = jnp.concatenate([mine] + [swap(mine, "col", 2 * m) for m in range(1, levels)], 0)
    stacks = [stack] + [None] * (rows - 1)
    for mask in far:
        stacks[mask] = swap(stack, "row", mask)
    stacks = stacks + [swap(value, "col", 1) for value in stacks]
    scen_adjoint, first_adjoint, coupling_grad = recover(
        rows, first_primal, scen_primal, own_cot, turned, blocks, stacks, width
    )
    return (scen_adjoint, first_adjoint, coupling_grad)


def solution(mesh):
    return jax.shard_map(
        body,
        mesh=mesh,
        in_specs=(
            P(("row", "col"), None, None),
            P(("row", "col"), None, None),
            P(("row", "col"), None, None),
            P("row", None),
            P("row", "col"),
            P(("row", "col"), None, None),
            P(),
        ),
        out_specs=(P(("row", "col"), None, None), P("col", None), P(("row", "col"), None, None)),
        check_vma=False,
    )
```

```python
import functools

import jax
import jax.numpy as jnp
from jax import lax
from jax.experimental import pallas as pl
from jax.experimental.pallas import tpu as pltpu
from jax.sharding import PartitionSpec as P

F32 = jnp.float32
BF16 = jnp.bfloat16
VMEM = pl.BlockSpec(memory_space=pltpu.VMEM)
ANY = pl.BlockSpec(memory_space=pl.ANY)
MIB = 1024 * 1024


def swap(value, axis, mask):
    size = lax.axis_size(axis)
    return lax.ppermute(value, axis, [(i, i ^ mask) for i in range(size)])


def cross(value, masks):
    rows, cols = lax.axis_size("row"), lax.axis_size("col")
    pairs = [(r * cols + c, (r ^ masks[c % 2]) * cols + c) for r in range(rows) for c in range(cols)]
    return lax.ppermute(value, ("row", "col"), pairs)


def turned_by(core, mask):
    return mask ^ (3 * (1 - core)) if lax.axis_size("row") == 4 and mask in (1, 2) else mask


def place():
    col = lax.axis_index("col")
    return lax.axis_index("row"), lax.rem(col, 2), lax.div(col, 2)


def dot(a, b):
    return jnp.dot(a, b, preferred_element_type=F32)


def dot_nt(a, b):
    return lax.dot_general(a, b, (((1,), (1,)), ((), ())), preferred_element_type=F32)


def dot_tn(a, b):
    return lax.dot_general(a, b, (((0,), (0,)), ((), ())), preferred_element_type=F32)


def condense_kernel(masks, first, *refs):
    row, core, _ = place()
    if first:
        inverse, cot, coupling, *refs = refs
        *outs, helper, own_inverse, own_cot, arrived = refs
    else:
        helper, coupling, *refs = refs
        *outs, arrived = refs
    keeps, gives, blocks = outs[0::3], outs[1::3], outs[2::3]
    count, size, depth = blocks[0].shape
    half = keeps[0].shape[0]
    copies = []
    if first:
        copies.append(pltpu.make_async_copy(cot, own_cot, arrived.at[0]))
        copies.append(pltpu.make_async_copy(inverse, own_inverse, arrived.at[1]))
    for i, mask in enumerate(masks):
        columns = pl.ds(pl.multiple_of((row ^ turned_by(core, mask)) * depth, 128), depth)
        copies.append(pltpu.make_async_copy(coupling.at[:, :, columns], blocks[i], arrived.at[2 + i]))
    for copy in copies:
        copy.start()
    if first:
        copies.pop(0).wait()
        copies.pop(0).wait()
        for s in range(count):
            value = dot_tn(own_cot[s], own_inverse[s]).astype(BF16)
            helper[core, :, s * size : (s + 1) * size] = value[:half]
            helper[1 - core, :, s * size : (s + 1) * size] = value[half:]
    left = helper[...].reshape(2 * half, count * size)
    for copy, keep, give, block in zip(copies, keeps, gives, blocks):
        copy.wait()
        value = dot(left, block[...].reshape(count * size, depth))
        keep[...] = value[:half]
        give[...] = value[half:].astype(BF16)


def condense(masks, inverse, cot, coupling, helper, depth):
    count, size, directions = cot.shape
    half = directions // 2
    first = helper is None
    outs = [pltpu.VMEM((half, depth), F32), pltpu.VMEM((half, depth), BF16), pltpu.VMEM((count, size, depth), BF16)]
    outs = outs * len(masks)
    inputs = [inverse, cot, coupling] if first else [coupling]
    inputs = [pltpu.with_memory_space_constraint(value, pltpu.HBM) for value in inputs]
    specs = [ANY] * len(inputs)
    if first:
        outs += [pltpu.VMEM((2, half, count * size), BF16)]
        outs += [pltpu.VMEM(inverse.shape, BF16), pltpu.VMEM(cot.shape, BF16)]
    else:
        inputs, specs = [helper] + inputs, [VMEM] + specs
    return pl.pallas_call(
        functools.partial(condense_kernel, masks, first),
        out_shape=outs,
        in_specs=specs,
        out_specs=[VMEM] * len(outs),
        scratch_shapes=[pltpu.SemaphoreType.DMA((2 + len(masks),))],
        compiler_params=pltpu.CompilerParams(vmem_limit_bytes=16 * MIB),
        cost_estimate=pl.CostEstimate(
            flops=2 * count * size * directions * depth * len(masks) if masks != [0] else 1024,
            bytes_accessed=(2 * len(masks)) << 20 if masks != [0] else 1024,
            transcendentals=0,
        ),
        name="condense",
    )(*inputs)


def prepare_kernel(schur, inverse, first_cot, high, low, turned, cot_half):
    half = cot_half.shape[0]
    value = schur[...].T
    top = value.astype(BF16)
    high[...] = top
    low[...] = (value - top.astype(F32)).astype(BF16)
    for s in range(inverse.shape[0]):
        turned[s] = inverse[s].astype(F32).T.astype(BF16)
    cot_half[...] = first_cot[:, pl.ds(pl.multiple_of(place()[1] * half, 128), half)].T


def prepare(schur, inverse, first_cot):
    depth, width = schur.shape
    split = pltpu.VMEM((width, depth), BF16)
    return pl.pallas_call(
        prepare_kernel,
        out_shape=[
            split,
            split,
            pltpu.VMEM(inverse.shape, BF16),
            pltpu.VMEM((first_cot.shape[1] // 2, depth), F32),
        ],
        in_specs=[VMEM, VMEM, VMEM],
        out_specs=[VMEM] * 4,
        compiler_params=pltpu.CompilerParams(vmem_limit_bytes=12 * MIB),
        cost_estimate=pl.CostEstimate(flops=1024, bytes_accessed=1024, transcendentals=0),
        name="prepare",
    )(schur, inverse, first_cot)


def product_kernel(masks, cot, total, last, high, low, high2, low2, *rest):
    outs, value = rest[:-1], rest[-1]
    row, core, _ = place()
    width = high.shape[0]
    part = outs[0].shape[0]
    right = cot[...] - (total[...] + last[...].astype(F32))
    top = right.astype(BF16)
    both = jnp.concatenate([top, (right - top.astype(F32)).astype(BF16)], 0)
    for at, (a, b) in ((core, (high, low)), (1 - core, (high2, low2))):
        wide = dot_nt(a[...], both)
        part_sum = wide[:, : wide.shape[1] // 2] + wide[:, wide.shape[1] // 2 :] + dot_nt(b[...], top)
        value[pl.ds(pl.multiple_of(at * width, 16), width), :] = part_sum
    for mask, out in zip(masks, outs):
        piece = value[pl.ds(pl.multiple_of((row ^ mask) * part, 16), part), :]
        out[...] = piece.astype(out.dtype)


def product(masks, cot, total, last, high, low, high2, low2):
    half, depth = cot.shape
    width = high.shape[0]
    part = 2 * width // len(masks)
    outs = [pltpu.VMEM((part, half), BF16 if mask else F32) for mask in masks]
    return pl.pallas_call(
        functools.partial(product_kernel, masks),
        out_shape=outs,
        in_specs=[VMEM] * 7,
        out_specs=[VMEM] * len(outs),
        scratch_shapes=[pltpu.VMEM((2 * width, half), F32)],
        compiler_params=pltpu.CompilerParams(vmem_limit_bytes=12 * MIB),
        cost_estimate=pl.CostEstimate(flops=12 * width * depth * half, bytes_accessed=4 << 20, transcendentals=0),
        name="product",
    )(cot, total, last, high, low, high2, low2)


def recover_kernel(rows, first_primal, primal, cot, turned, *rest):
    blocks, rest = rest[:rows], rest[rows:]
    stacks, rest = rest[: 2 * rows], rest[2 * rows :]
    scen_adjoint, first_adjoint, grad, right, left, primals, update, adjoints, firsts, tile, arrived, gone = rest
    row, core, level = place()
    count, size, depth = blocks[0].shape
    total, directions = first_primal.shape
    half = directions // 2
    width = first_adjoint.shape[0]
    part = 2 * width // rows
    levels = stacks[0].shape[0] // part
    loads = [
        pltpu.make_async_copy(first_primal, right.at[:, pl.ds(0, directions)], arrived.at[0]),
        pltpu.make_async_copy(primal, primals, arrived.at[1]),
    ]
    for load in loads:
        load.start()
    for side in range(2):
        lanes = pl.ds(pl.multiple_of(directions + (core ^ side) * half, 128), half)
        for mask in range(rows):
            for step in range(levels):
                start = (level ^ step) * (2 * width) + (row ^ mask) * part
                piece = stacks[side * rows + mask][step * part : (step + 1) * part, :]
                right[pl.ds(pl.multiple_of(start, 16), part), lanes] = piece
    stores = []

    def store(source, target):
        stores.append(pltpu.make_async_copy(source, target, gone.at[len(stores)]))
        stores[-1].start()

    start = pl.multiple_of((level * 2 + core) * width, 16)
    firsts[...] = right[pl.ds(start, width), directions:].astype(F32)
    store(firsts, first_adjoint)
    for s in range(count):
        value = cot[s].astype(F32)
        for mask in range(rows):
            start = pl.multiple_of((row ^ turned_by(core, mask)) * depth, 128)
            value = value - dot(blocks[mask][s], right[pl.ds(start, depth), directions:])
        update[...] = value.astype(BF16)
        value = dot(turned[s], update[...])
        adjoints[s] = value
        store(adjoints.at[s], scen_adjoint.at[s])
        left[:, :directions] = -value.astype(BF16)
        if s == 0:
            for load in loads:
                load.wait()
        left[:, directions:] = -primals[s]
        for i in range(rows):
            slot = s * rows + i
            tile[slot] = dot_nt(left[...], right[i * depth : (i + 1) * depth, :])
            store(tile.at[slot], grad.at[s, :, pl.ds(i * depth, depth)])
    for copy in stores:
        copy.wait()


def recover(rows, first_primal, primal, cot, turned, blocks, stacks, width):
    count, size, depth = blocks[0].shape
    total, directions = first_primal.shape
    outs = [
        jax.ShapeDtypeStruct(cot.shape, F32),
        jax.ShapeDtypeStruct((width, directions), F32),
        jax.ShapeDtypeStruct((count, size, total), F32),
    ]
    inputs = [pltpu.with_memory_space_constraint(value, pltpu.HBM) for value in (first_primal, primal)]
    return pl.pallas_call(
        functools.partial(recover_kernel, rows),
        out_shape=outs,
        in_specs=[ANY, ANY] + [VMEM] * (2 + len(blocks) + len(stacks)),
        out_specs=[ANY, ANY, ANY],
        scratch_shapes=[
            pltpu.VMEM((total, 2 * directions), BF16),
            pltpu.VMEM((size, 2 * directions), BF16),
            pltpu.VMEM(primal.shape, BF16),
            pltpu.VMEM((size, directions), BF16),
            pltpu.VMEM(cot.shape, F32),
            pltpu.VMEM((width, directions), F32),
            pltpu.VMEM((count * rows, size, depth), F32),
            pltpu.SemaphoreType.DMA((2,)),
            pltpu.SemaphoreType.DMA((1 + count * (1 + rows),)),
        ],
        compiler_params=pltpu.CompilerParams(vmem_limit_bytes=28 * MIB),
        cost_estimate=pl.CostEstimate(
            flops=2 * count * size * directions * (3 * total + size), bytes_accessed=20 << 20, transcendentals=0
        ),
        name="recover",
    )(*inputs, cot, turned, *blocks, *stacks)


def body(scen_inverse, coupling, scen_cot, first_cot, schur_inverse, scen_primal, first_primal):
    rows, cols = lax.axis_size("row"), lax.axis_size("col")
    levels = cols // 2
    depth, width = schur_inverse.shape
    far = sorted(range(1, rows), key=lambda m: -bin(m).count("1"))

    blocks = [None] * rows
    outs = condense(far, scen_inverse, scen_cot, coupling, None, depth)
    helper, own_inverse, own_cot = outs[-3:]
    keeps, gives = [None] * rows, [None] * rows
    for i, mask in enumerate(far):
        keeps[mask], gives[mask], blocks[mask] = outs[3 * i : 3 * i + 3]

    def chip(mask):
        return keeps[mask] + swap(gives[int(turned_by(0, mask))], "col", 1).astype(F32)

    terms = {mask: chip(mask) for mask in far}
    ready = {mask: terms[mask].astype(BF16) for mask in far}
    helper, *values = lax.optimization_barrier((helper, *ready.values()))
    ready = dict(zip(far, values))
    keeps[0], gives[0], blocks[0] = condense([0], scen_inverse, scen_cot, coupling, helper, depth)
    total = chip(0)
    if rows == 4:
        through = cross(ready[3], (2, 1))
        near = cross(ready[1], (2, 1))
        passed = (terms[2] + through.astype(F32)).astype(BF16)
        own_inverse, passed = lax.optimization_barrier((own_inverse, passed))
        arrived = [near, cross(passed, (1, 2))]
    else:
        arrived = [swap(ready[mask], "row", mask) for mask in far]
    for value in arrived:
        total = total + value.astype(F32)

    high, low, turned, cot_half = prepare(schur_inverse, own_inverse, first_cot)
    total, high, low, turned, cot_half = lax.optimization_barrier((total, high, low, turned, cot_half))
    high2, low2 = swap(high, "col", 1), swap(low, "col", 1)

    mask = 2
    last = None
    while mask < cols:
        if last is not None:
            total = total + last.astype(F32)
        last = swap(total.astype(BF16), "col", mask if 2 * mask < cols else cols - 2)
        mask *= 2

    pieces = product([0] + far, cot_half, total, last, high, low, high2, low2)
    mine = pieces[0]
    for mask, piece in zip(far, pieces[1:]):
        mine = mine + swap(piece, "row", mask).astype(F32)
    mine = mine.astype(BF16)

    stack = jnp.concatenate([mine] + [swap(mine, "col", 2 * m) for m in range(1, levels)], 0)
    stacks = [stack] + [None] * (rows - 1)
    for mask in far:
        stacks[mask] = swap(stack, "row", mask)
    stacks = stacks + [swap(value, "col", 1) for value in stacks]
    scen_adjoint, first_adjoint, coupling_grad = recover(
        rows, first_primal, scen_primal, own_cot, turned, blocks, stacks, width
    )
    return (scen_adjoint, first_adjoint, coupling_grad)


def solution(mesh):
    return jax.shard_map(
        body,
        mesh=mesh,
        in_specs=(
            P(("row", "col"), None, None),
            P(("row", "col"), None, None),
            P(("row", "col"), None, None),
            P("row", None),
            P("row", "col"),
            P(("row", "col"), None, None),
            P(),
        ),
        out_specs=(P(("row", "col"), None, None), P("col", None), P(("row", "col"), None, None)),
        check_vma=False,
    )
```
